128 devices in a mesh: rows: 8 (over y_hi, x), cols: 16 (over y_lo, z, core).
Axes of the slice: x: 4, y: 4 (y_hi: 2, y_lo: 2; y = y_hi * 2 + y_lo), z: 4, core: 2. Of those that a mesh axis runs over, the one named last changes fastest.
Arguments:
- entities: bfloat16 [16384, 4096], P('rows', 'cols'), may hold values from -20 to 20, as said below
- start_basis: float32 [4096, 512], P('cols'), may hold values from -0.09375 to 0.09375
Outputs:
- compressed: bfloat16 [16384, 512], P('rows', 'cols')
The draws below stay inside these ranges and needn't reach their ends.
Inputs may be any that keep to these rules, and one draw needn't show every extreme that they name: `entities`: real-valued embedding entries.
All inputs are finite; a program needn't handle non-finite values.
Results may differ from the reference program's by a relative error of at most 0.0042.
Values may be sent and summed in bfloat16 or wider, within the bound.
No kernel may reach another device: no remote copies, remote signals or barrier semaphores. Data moves between devices by JAX's collectives and lax.ppermute only.
A program may use at most 128 MiB of HBM per device.

```python
import math
import jax
import jax.numpy as jnp
from jax import lax

D = 4096
K = 512
ITERS = 2
TOTAL = 16384


def draw_entities(key, part):
    key = jax.random.fold_in(key, 1)
    key_noise, key_row, key_col = jax.random.split(key, 3)
    noise = jnp.clip(jax.random.normal(key_noise, (TOTAL, D), jnp.float32), -5.0, 5.0)
    row_low, row_high, col_low, col_high = (0.5, 2.0, 0.75, 1.33)
    row_scale = jnp.exp(jax.random.uniform(key_row, (TOTAL, 1), jnp.float32, math.log(row_low), math.log(row_high)))
    col_scale = jnp.exp(jax.random.uniform(key_col, (1, D), jnp.float32, math.log(col_low), math.log(col_high)))
    return (noise * row_scale * col_scale).astype(jnp.bfloat16)


def level_of(rng, extent, cuts, least, top_value):
    def one(axis_at, shards_of):
        heights = jax.random.uniform(jax.random.fold_in(jax.random.fold_in(rng, 6), axis_at), (shards_of,), jnp.float32, least / len(cuts), top_value / len(cuts))
        return jnp.repeat(jnp.exp(heights), extent[axis_at] // shards_of).reshape((-1,) + (1,) * (len(extent) - axis_at - 1))

    loudness = one(*cuts[0])
    for cut in cuts[1:]:
        loudness = loudness * one(*cut)
    return loudness


def gaussian(rng, dims, deviation, reach, pieces=(), dtype=jnp.bfloat16):
    gain = level_of(rng, dims, pieces, -0.22, 0.18) if pieces else 1.0
    entries = jax.random.normal(rng, dims, jnp.float32) * deviation * gain
    return jnp.minimum(jnp.maximum(entries, -reach), reach).astype(dtype)


def setup_inputs(seed: int = 0) -> dict:
    streams_of = jax.random.split(jax.random.key(seed), 3)
    entities = draw_entities(jax.random.fold_in(streams_of[2], 71), 0)
    start_basis = gaussian(streams_of[1], (D, K), D ** -0.5, 0.09375, ((0, 16),), jnp.float32)
    return {"entities": entities, "start_basis": start_basis}


def reference(entities, start_basis):
    covariance = jnp.dot(entities.T.astype(jnp.float32), entities.astype(jnp.float32), preferred_element_type=jnp.float32) / TOTAL
    current = start_basis
    for step in range(ITERS):
        image = jnp.dot(covariance, current, precision=lax.Precision.HIGHEST)
        gram = jnp.dot(image.T, image, precision=lax.Precision.HIGHEST)
        lower = jnp.linalg.cholesky(gram)
        current = jax.scipy.linalg.solve_triangular(lower, image.T, lower=True).T
    rounded = current.astype(jnp.bfloat16)
    return jnp.dot(entities.astype(jnp.float32), rounded.astype(jnp.float32), preferred_element_type=jnp.float32).astype(jnp.bfloat16)
```

```python
import jax
import jax.numpy as jnp
from jax import lax
from jax.experimental import pallas as pl
from jax.experimental.pallas import tpu as pltpu
from jax.sharding import Mesh, PartitionSpec as P

ITERS = 2
ROWS = ("y_hi", "x")
PLANE = ("y_lo", "z")
COLS = ("y_lo", "z", "core")
HIGHEST = lax.Precision.HIGHEST
VMEM_LIMIT = 48 * 2**20
MIDDLE = 32


def full_dot(a, b, contract):
    return lax.dot_general(
        a, b, (contract, ((), ())), precision=HIGHEST, preferred_element_type=jnp.float32
    )


def spread(x):
    return jnp.broadcast_to(x, (8, 128))


def eliminate(left, right, col):
    top, top_right = left[0], right[0]
    s = [[spread(top[i : i + 1, col + j : col + j + 1]) if j >= i else None for j in range(8)] for i in range(8)]
    rows_left = [spread(top[i : i + 1, :]) for i in range(8)]
    rows_right = [spread(top_right[i : i + 1, :]) for i in range(8)]
    inverse = []
    for j in range(8):
        inverse.append(1.0 / s[j][j])
        for i in range(j + 1, 8):
            factor = s[j][i] * inverse[j]
            for k in range(i, 8):
                s[i][k] = s[i][k] - factor * s[j][k]
            rows_left[i] = rows_left[i] - factor * rows_left[j]
            rows_right[i] = rows_right[i] - factor * rows_right[j]
    row = lax.broadcasted_iota(jnp.int32, (8, 128), 0)
    done_left, done_right, scale = rows_left[0], rows_right[0], inverse[0]
    for i in range(1, 8):
        done_left = jnp.where(row == i, rows_left[i], done_left)
        done_right = jnp.where(row == i, rows_right[i], done_right)
        scale = jnp.where(row == i, inverse[i], scale)
    new_left, new_right = [], []
    for x, y in zip(left[1:], right[1:]):
        c = [spread(x[:, col + j : col + j + 1]) for j in range(8)]
        for j in range(8):
            factor = c[j] * inverse[j]
            for k in range(j + 1, 8):
                c[k] = c[k] - factor * s[j][k]
            x = x - factor * rows_left[j]
            y = y - factor * rows_right[j]
        new_left.append(x)
        new_right.append(y)
    return done_left, done_right, scale, new_left, new_right


def invert_block(a):
    rows = lax.broadcasted_iota(jnp.int32, (128, 128), 0)
    cols = lax.broadcasted_iota(jnp.int32, (128, 128), 1)
    v = jnp.where(rows == cols, 1.0, 0.0).astype(jnp.float32)
    out = []
    for m in range(0, 128, MIDDLE):
        left = [a[i : i + 8, :] for i in range(0, MIDDLE, 8)]
        right = [v[i : i + 8, :] for i in range(0, MIDDLE, 8)]
        lefts, rights, scales = [], [], []
        for g in range(MIDDLE // 8):
            done_left, done_right, scale, left, right = eliminate(left, right, m + 8 * g)
            lefts.append(done_left)
            rights.append(done_right)
            scales.append(scale)
        u, w, d = jnp.concatenate(lefts, 0), jnp.concatenate(rights, 0), jnp.concatenate(scales, 0)
        out.append(w * jnp.sqrt(d))
        if m + MIDDLE < 128:
            factors = (u * d)[:, m + MIDDLE :]
            a = a[MIDDLE:] - full_dot(factors, u, ((0,), (0,)))
            v = v[MIDDLE:] - full_dot(factors, w, ((0,), (0,)))
    return jnp.concatenate(out, 0)


def inverse_factor_kernel(gram_ref, out_ref, a_ref):
    n = gram_ref.shape[0]
    a_ref[...] = gram_ref[...]
    out_ref[...] = jnp.zeros_like(out_ref)
    for k in range(0, n, 128):
        block = slice(k, k + 128)
        w = invert_block(a_ref[block, block])
        if k:
            out_ref[block, :k] = full_dot(w, out_ref[block, :k], ((1,), (0,)))
        out_ref[block, block] = w
        if k + 128 < n:
            u = full_dot(w, a_ref[block, k + 128 :], ((1,), (0,)))
            a_ref[k + 128 :, k + 128 :] -= full_dot(u, u, ((0,), (0,)))
            out_ref[k + 128 :, : k + 128] -= full_dot(u, out_ref[block, : k + 128], ((0,), (0,)))


def inverse_factor(gram):
    n = gram.shape[0]
    return pl.pallas_call(
        inverse_factor_kernel,
        out_shape=jax.ShapeDtypeStruct((n, n), jnp.float32),
        in_specs=[pl.BlockSpec(memory_space=pltpu.VMEM)],
        out_specs=pl.BlockSpec(memory_space=pltpu.VMEM),
        scratch_shapes=[pltpu.VMEM((n, n), jnp.float32)],
        compiler_params=pltpu.CompilerParams(vmem_limit_bytes=VMEM_LIMIT),
        cost_estimate=pl.CostEstimate(flops=20 * n**3, bytes_accessed=8 * n * n, transcendentals=n),
        name="inverse_factor",
    )(gram)


def three_parts(x):
    high = x.astype(jnp.bfloat16)
    rest = x - high.astype(jnp.float32)
    middle = rest.astype(jnp.bfloat16)
    low = (rest - middle.astype(jnp.float32)).astype(jnp.bfloat16)
    return jnp.concatenate([high, middle, low], 0)


def forward_kernel(order_ref, basis_ref, entities_ref, out_ref, parts_ref):
    blocks, width = basis_ref.shape[:2]
    split = basis_ref.dtype == jnp.float32

    @pl.when(pl.program_id(0) == 0)
    def _():
        for k in range(blocks):
            block = basis_ref[order_ref[k]]
            parts_ref[k] = three_parts(block) if split else block

    total = 0.0
    for k in range(blocks):
        total += lax.dot_general(
            parts_ref[k], entities_ref[k], (((1,), (1,)), ((), ())), preferred_element_type=jnp.float32
        )
    if split:
        total = total[:width] + total[width : 2 * width] + total[2 * width :]
    out_ref[...] = total


def forward(order, basis, entities):
    blocks, width, features = basis.shape
    rows = entities.shape[1]
    tile = 256
    parts = 3 if basis.dtype == jnp.float32 else 1
    return pl.pallas_call(
        forward_kernel,
        out_shape=jax.ShapeDtypeStruct((width, rows), jnp.float32),
        grid_spec=pltpu.PrefetchScalarGridSpec(
            num_scalar_prefetch=1,
            grid=(rows // tile,),
            in_specs=[
                pl.BlockSpec((blocks, width, features), lambda i, order: (0, 0, 0)),
                pl.BlockSpec((blocks, tile, features), lambda i, order: (0, i, 0)),
            ],
            out_specs=pl.BlockSpec((width, tile), lambda i, order: (0, i)),
            scratch_shapes=[pltpu.VMEM((blocks, parts * width, features), jnp.bfloat16)],
        ),
        compiler_params=pltpu.CompilerParams(vmem_limit_bytes=VMEM_LIMIT),
        cost_estimate=pl.CostEstimate(
            flops=8 * rows * width * blocks * features, bytes_accessed=entities.size * 2, transcendentals=0
        ),
        name="forward",
    )(order, basis, entities)


def backward_kernel(order_ref, mine_ref, other_ref, entities_ref, out_ref, parts_ref):
    width = mine_ref.shape[0]

    @pl.when(pl.program_id(0) == 0)
    def _():
        parts_ref[...] = three_parts(mine_ref[...] + other_ref[...])

    total = jnp.dot(parts_ref[...], entities_ref[0], preferred_element_type=jnp.float32)
    out_ref[0] = total[:width] + total[width : 2 * width] + total[2 * width :]


def backward(order, mine, other, entities):
    blocks, rows, features = entities.shape
    width = mine.shape[0]
    return pl.pallas_call(
        backward_kernel,
        out_shape=jax.ShapeDtypeStruct((blocks, width, features), jnp.float32),
        grid_spec=pltpu.PrefetchScalarGridSpec(
            num_scalar_prefetch=1,
            grid=(blocks,),
            in_specs=[
                pl.BlockSpec((width, rows), lambda i, order: (0, 0)),
                pl.BlockSpec((width, rows), lambda i, order: (0, 0)),
                pl.BlockSpec((1, rows, features), lambda i, order: (i, 0, 0)),
            ],
            out_specs=pl.BlockSpec((1, width, features), lambda i, order: (order[i], 0, 0)),
            scratch_shapes=[pltpu.VMEM((3 * width, rows), jnp.bfloat16)],
        ),
        compiler_params=pltpu.CompilerParams(vmem_limit_bytes=VMEM_LIMIT),
        cost_estimate=pl.CostEstimate(
            flops=8 * rows * width * blocks * features, bytes_accessed=entities.size * 2, transcendentals=0
        ),
        name="backward",
    )(order, mine, other, entities)


def exchange(x, axes):
    return lax.all_to_all(x, axes, 0, 0, tiled=True)


def gather(x, axes):
    peers = lax.axis_size(axes)
    return exchange(jnp.broadcast_to(x[None], (peers,) + x.shape), axes)


def swap(x, axis):
    return lax.ppermute(x, axis, [(0, 1), (1, 0)])


def shift(x, step):
    n = lax.axis_size("z")
    return lax.ppermute(x, "z", [(i, (i + step) % n) for i in range(n)])


def gather_entities(x):
    half = x.shape[0] // 2
    quarter = half // 2
    before, after = shift(x, 1), shift(x, -1)
    across = swap(x, "y_lo")
    far_top, far_low = shift(before[:half], 1), shift(after[half:], -1)
    before_top, after_top = swap(before[:half], "y_lo"), swap(after[:half], "y_lo")
    before_low, after_low = shift(across[half:], 1), shift(across[half:], -1)
    across_far_top = swap(far_top, "y_lo")
    across_far_mid = shift(before_low[:quarter], 1)
    across_far_low = shift(after_low[quarter:], -1)
    pieces = [
        x, before, after, far_top, far_low, across, before_top, before_low,
        after_top, after_low, across_far_top, across_far_mid, across_far_low,
    ]
    return jnp.concatenate(pieces, 0).reshape(8, x.shape[0], x.shape[1])


def whole_gram(block, place, core):
    width = block.shape[0] // 8
    mine = lax.dynamic_slice_in_dim(block, place * width, width, 0)
    part = full_dot(mine, block, ((1,), (1,)))
    half = width // 2
    keep = lax.dynamic_slice_in_dim(part, core * half, half, 0)
    give = lax.dynamic_slice_in_dim(part, (1 - core) * half, half, 0)
    part = keep + swap(give, "core")
    part = jnp.sum(gather(part, ROWS), 0)
    return gather(part, COLS).reshape(block.shape[0], block.shape[0])


def local(entities, start_basis):
    rows, features = entities.shape
    total_rows = rows * lax.axis_size(ROWS)
    width = start_basis.shape[1] // 8
    y_lo, z, core = (lax.axis_index(a) for a in COLS)
    place = y_lo * 4 + z
    line = jnp.stack([z, (z + 3) % 4, (z + 1) % 4, (z + 2) % 4])
    order = jnp.concatenate([y_lo * 4 + line, (1 - y_lo) * 4 + line]).astype(jnp.int32)

    basis = exchange(start_basis.T.reshape(8, width, features), PLANE)
    gathered = gather_entities(entities)

    def covariance_times(basis):
        part = forward(order, basis, gathered)
        sums = backward(order, part, swap(part, "core"), gathered)
        return jnp.sum(exchange(sums, ROWS), 0) / total_rows

    image = covariance_times(basis)
    block = gather(image, PLANE).reshape(8 * width, features)
    for step in range(ITERS):
        if step + 1 < ITERS:
            image = covariance_times(gather(image, ROWS))
            following = gather(image, PLANE).reshape(8 * width, features)
        inverse = inverse_factor(whole_gram(block, place, core))
        if step + 1 < ITERS:
            block = full_dot(inverse, following, ((1,), (0,)))
    current = full_dot(lax.dynamic_slice_in_dim(inverse, place * width, width, 0), block, ((1,), (0,)))
    rounded = current.astype(jnp.bfloat16)
    part = forward(order, gather(rounded, ROWS), gathered)
    half = width // 2
    keep = lax.dynamic_slice_in_dim(part, core * half, half, 0)
    give = lax.dynamic_slice_in_dim(part, (1 - core) * half, half, 0)
    return (keep + swap(give, "core")).T.astype(jnp.bfloat16)


def solution(mesh):
    fine = Mesh(mesh.devices.reshape(2, 4, 2, 4, 2), ROWS + COLS)
    return jax.shard_map(
        local,
        mesh=fine,
        in_specs=(P(ROWS, COLS), P(COLS, None)),
        out_specs=P(ROWS, COLS),
        check_vma=False,
    )
```

```python
import jax
import jax.numpy as jnp
from jax import lax
from jax.experimental import pallas as pl
from jax.experimental.pallas import tpu as pltpu
from jax.sharding import Mesh, PartitionSpec as P

ITERS = 2
ROWS = ("y_hi", "x")
PLANE = ("y_lo", "z")
COLS = ("y_lo", "z", "core")
HIGHEST = lax.Precision.HIGHEST
VMEM_LIMIT = 16 * 2**20
MIDDLE = 32


def full_dot(a, b, contract):
    return lax.dot_general(
        a, b, (contract, ((), ())), precision=HIGHEST, preferred_element_type=jnp.float32
    )


def spread(x):
    return jnp.broadcast_to(x, (8, 128))


def eliminate(left, right, col):
    top, top_right = left[0], right[0]
    s = [[spread(top[i : i + 1, col + j : col + j + 1]) if j >= i else None for j in range(8)] for i in range(8)]
    rows_left = [spread(top[i : i + 1, :]) for i in range(8)]
    rows_right = [spread(top_right[i : i + 1, :]) for i in range(8)]
    inverse = []
    for j in range(8):
        inverse.append(1.0 / s[j][j])
        for i in range(j + 1, 8):
            factor = s[j][i] * inverse[j]
            for k in range(i, 8):
                s[i][k] = s[i][k] - factor * s[j][k]
            rows_left[i] = rows_left[i] - factor * rows_left[j]
            rows_right[i] = rows_right[i] - factor * rows_right[j]
    row = lax.broadcasted_iota(jnp.int32, (8, 128), 0)
    done_left, done_right, scale = rows_left[0], rows_right[0], inverse[0]
    for i in range(1, 8):
        done_left = jnp.where(row == i, rows_left[i], done_left)
        done_right = jnp.where(row == i, rows_right[i], done_right)
        scale = jnp.where(row == i, inverse[i], scale)
    new_left, new_right = [], []
    for x, y in zip(left[1:], right[1:]):
        c = [spread(x[:, col + j : col + j + 1]) for j in range(8)]
        for j in range(8):
            factor = c[j] * inverse[j]
            for k in range(j + 1, 8):
                c[k] = c[k] - factor * s[j][k]
            x = x - factor * rows_left[j]
            y = y - factor * rows_right[j]
        new_left.append(x)
        new_right.append(y)
    return done_left, done_right, scale, new_left, new_right


def invert_block(a):
    rows = lax.broadcasted_iota(jnp.int32, (128, 128), 0)
    cols = lax.broadcasted_iota(jnp.int32, (128, 128), 1)
    v = jnp.where(rows == cols, 1.0, 0.0).astype(jnp.float32)
    out = []
    for m in range(0, 128, MIDDLE):
        left = [a[i : i + 8, :] for i in range(0, MIDDLE, 8)]
        right = [v[i : i + 8, :] for i in range(0, MIDDLE, 8)]
        lefts, rights, scales = [], [], []
        for g in range(MIDDLE // 8):
            done_left, done_right, scale, left, right = eliminate(left, right, m + 8 * g)
            lefts.append(done_left)
            rights.append(done_right)
            scales.append(scale)
        u, w, d = jnp.concatenate(lefts, 0), jnp.concatenate(rights, 0), jnp.concatenate(scales, 0)
        out.append(w * jnp.sqrt(d))
        if m + MIDDLE < 128:
            factors = (u * d)[:, m + MIDDLE :]
            a = a[MIDDLE:] - full_dot(factors, u, ((0,), (0,)))
            v = v[MIDDLE:] - full_dot(factors, w, ((0,), (0,)))
    return jnp.concatenate(out, 0)


def inverse_factor_kernel(core_ref, mine_ref, other_ref, out_ref, a_ref):
    n = out_ref.shape[0]
    blocks, half = mine_ref.shape[:2]
    for i in range(blocks):
        base = 2 * half * i
        a_ref[pl.ds(pl.multiple_of(base + core_ref[0] * half, 8), half), :] = mine_ref[i]
        a_ref[pl.ds(pl.multiple_of(base + (1 - core_ref[0]) * half, 8), half), :] = other_ref[i]
    out_ref[...] = jnp.zeros_like(out_ref)
    for k in range(0, n, 128):
        block = slice(k, k + 128)
        w = invert_block(a_ref[block, block])
        if k:
            out_ref[block, :k] = full_dot(w, out_ref[block, :k], ((1,), (0,)))
        out_ref[block, block] = w
        if k + 128 < n:
            u = full_dot(w, a_ref[block, k + 128 :], ((1,), (0,)))
            a_ref[k + 128 :, k + 128 :] -= full_dot(u, u, ((0,), (0,)))
            out_ref[k + 128 :, : k + 128] -= full_dot(u, out_ref[block, : k + 128], ((0,), (0,)))


IN_VMEM = pl.BlockSpec(memory_space=pltpu.VMEM)
IN_SMEM = pl.BlockSpec(memory_space=pltpu.SMEM)


def inverse_factor(core, mine, other):
    n = mine.shape[2]
    return pl.pallas_call(
        inverse_factor_kernel,
        out_shape=jax.ShapeDtypeStruct((n, n), jnp.float32),
        in_specs=[IN_SMEM, IN_VMEM, IN_VMEM],
        out_specs=IN_VMEM,
        scratch_shapes=[pltpu.VMEM((n, n), jnp.float32)],
        compiler_params=pltpu.CompilerParams(vmem_limit_bytes=VMEM_LIMIT),
        cost_estimate=pl.CostEstimate(flops=200 * n**3, bytes_accessed=8 * n * n, transcendentals=n),
        name="inverse_factor",
    )(core.reshape(1), mine, other)


PIECES = [
    (0, 0, 4), (1, 0, 4), (2, 0, 4), (3, 0, 2), (3, 2, 2), (4, 0, 4), (5, 0, 2),
    (5, 2, 2), (6, 0, 2), (6, 2, 2), (7, 0, 2), (7, 2, 1), (7, 3, 1),
]


def three_parts(x):
    high = x.astype(jnp.bfloat16)
    rest = x - high.astype(jnp.float32)
    middle = rest.astype(jnp.bfloat16)
    low = (rest - middle.astype(jnp.float32)).astype(jnp.bfloat16)
    return jnp.concatenate([high, middle, low], 0)


def add_parts(total, width):
    return total[:width] + total[width : 2 * width] + total[2 * width :]


def forward_kernel(order_ref, basis_ref, *refs):
    pieces, out_ref, weights_ref = refs[:-2], refs[-2], refs[-1]
    blocks, width, _ = basis_ref.shape
    split = basis_ref.dtype == jnp.float32
    tile = out_ref.shape[1] // 4
    for k in range(blocks):
        block = basis_ref[order_ref[k]]
        weights_ref[k] = (three_parts(block) if split else block).T
    for quarter in range(4):
        total = 0.0
        for piece, (k, first, count) in zip(pieces, PIECES):
            if first <= quarter < first + count:
                rows = slice((quarter - first) * tile, (quarter - first + 1) * tile)
                total += jnp.dot(piece[rows, :], weights_ref[k], preferred_element_type=jnp.float32)
        total = total.T
        out_ref[:, quarter * tile : (quarter + 1) * tile] = add_parts(total, width) if split else total


def forward(order, basis, pieces):
    blocks, width, features = basis.shape
    rows = pieces[0].shape[0]
    parts = 3 if basis.dtype == jnp.float32 else 1
    return pl.pallas_call(
        forward_kernel,
        out_shape=jax.ShapeDtypeStruct((width, rows), jnp.float32),
        in_specs=[IN_SMEM] + [IN_VMEM] * (1 + len(pieces)),
        out_specs=IN_VMEM,
        scratch_shapes=[pltpu.VMEM((blocks, features, parts * width), jnp.bfloat16)],
        compiler_params=pltpu.CompilerParams(vmem_limit_bytes=VMEM_LIMIT),
        cost_estimate=pl.CostEstimate(
            flops=16 * rows * width * blocks * features, bytes_accessed=2 * width * rows, transcendentals=0
        ),
        name="forward",
    )(order, basis, *pieces)


def backward_kernel(order_ref, mine_ref, other_ref, *refs):
    pieces, out_ref, parts_ref = refs[:-2], refs[-2], refs[-1]
    width, rows = mine_ref.shape
    parts_ref[...] = three_parts(mine_ref[...] + other_ref[...])
    for block in range(out_ref.shape[0]):
        total = 0.0
        for piece, (k, first, count) in zip(pieces, PIECES):
            if k == block:
                at = slice(first * rows // 4, (first + count) * rows // 4)
                total += jnp.dot(parts_ref[:, at], piece[...], preferred_element_type=jnp.float32)
        out_ref[order_ref[block]] = add_parts(total, width)


def backward(order, mine, other, pieces):
    width, rows = mine.shape
    blocks, features = order.shape[0], pieces[0].shape[1]
    return pl.pallas_call(
        backward_kernel,
        out_shape=jax.ShapeDtypeStruct((blocks, width, features), jnp.float32),
        in_specs=[IN_SMEM] + [IN_VMEM] * (2 + len(pieces)),
        out_specs=IN_VMEM,
        scratch_shapes=[pltpu.VMEM((3 * width, rows), jnp.bfloat16)],
        compiler_params=pltpu.CompilerParams(vmem_limit_bytes=VMEM_LIMIT),
        cost_estimate=pl.CostEstimate(
            flops=16 * rows * width * blocks * features, bytes_accessed=2 * width * rows, transcendentals=0
        ),
        name="backward",
    )(order, mine, other, *pieces)


def exchange(x, axes):
    return lax.all_to_all(x, axes, 0, 0, tiled=True)


def gather(x, axes):
    peers = lax.axis_size(axes)
    return exchange(jnp.broadcast_to(x[None], (peers,) + x.shape), axes)


def swap(x, axis):
    return lax.ppermute(x, axis, [(0, 1), (1, 0)])


def shift(x, step):
    n = lax.axis_size("z")
    return lax.ppermute(x, "z", [(i, (i + step) % n) for i in range(n)])


def gather_entities(x):
    half = x.shape[0] // 2
    quarter = half // 2
    before, after = shift(x, 1), shift(x, -1)
    across = swap(x, "y_lo")
    far_top, far_low = shift(before[:half], 1), shift(after[half:], -1)
    before_top, after_top = swap(before[:half], "y_lo"), swap(after[:half], "y_lo")
    before_low, after_low = shift(across[half:], 1), shift(across[half:], -1)
    across_far_top = swap(far_top, "y_lo")
    across_far_mid = shift(before_low[:quarter], 1)
    across_far_low = shift(after_low[quarter:], -1)
    return [
        x, before, after, far_top, far_low, across, before_top, before_low,
        after_top, after_low, across_far_top, across_far_mid, across_far_low,
    ]


def whole_gram(block, place, core):
    width = block.shape[0] // 8
    mine = lax.dynamic_slice_in_dim(block, place * width, width, 0)
    part = full_dot(mine, block, ((1,), (1,)))
    half = width // 2
    keep = lax.dynamic_slice_in_dim(part, core * half, half, 0)
    give = lax.dynamic_slice_in_dim(part, (1 - core) * half, half, 0)
    part = keep + swap(give, "core")
    part = jnp.sum(gather(part, ROWS), 0)
    part = gather(part, PLANE)
    return part, swap(part, "core")


def local(entities, start_basis):
    rows, features = entities.shape
    total_rows = rows * lax.axis_size(ROWS)
    width = start_basis.shape[1] // 8
    y_lo, z, core = (lax.axis_index(a) for a in COLS)
    place = y_lo * 4 + z
    line = jnp.stack([z, (z + 3) % 4, (z + 1) % 4, (z + 2) % 4])
    order = jnp.concatenate([y_lo * 4 + line, (1 - y_lo) * 4 + line]).astype(jnp.int32)

    basis = exchange(start_basis.T.reshape(8, width, features), PLANE)
    gathered = gather_entities(entities)

    def covariance_times(basis):
        part = forward(order, basis, gathered)
        sums = backward(order, part, swap(part, "core"), gathered)
        return jnp.sum(exchange(sums, ROWS), 0) / total_rows

    image = covariance_times(basis)
    block = gather(image, PLANE).reshape(8 * width, features)
    for step in range(ITERS):
        if step + 1 < ITERS:
            image = covariance_times(gather(image, ROWS))
            following = gather(image, PLANE).reshape(8 * width, features)
        inverse = inverse_factor(core, *whole_gram(block, place, core))
        if step + 1 < ITERS:
            block = full_dot(inverse, following, ((1,), (0,)))
    current = full_dot(lax.dynamic_slice_in_dim(inverse, place * width, width, 0), block, ((1,), (0,)))
    rounded = current.astype(jnp.bfloat16)
    part = forward(order, gather(rounded, ROWS), gathered)
    half = width // 2
    keep = lax.dynamic_slice_in_dim(part, core * half, half, 0)
    give = lax.dynamic_slice_in_dim(part, (1 - core) * half, half, 0)
    return (keep + swap(give, "core")).T.astype(jnp.bfloat16)


def solution(mesh):
    fine = Mesh(mesh.devices.reshape(2, 4, 2, 4, 2), ROWS + COLS)
    return jax.shard_map(
        local,
        mesh=fine,
        in_specs=(P(ROWS, COLS), P(COLS, None)),
        out_specs=P(ROWS, COLS),
        check_vma=False,
    )
```

```python
import functools

import jax
import jax.numpy as jnp
from jax import lax
from jax.experimental import pallas as pl
from jax.experimental.pallas import tpu as pltpu
from jax.sharding import Mesh, PartitionSpec as P

ITERS = 2
ROWS = ("y_hi", "x")
PLANE = ("y_lo", "z")
COLS = ("y_lo", "z", "core")
HIGHEST = lax.Precision.HIGHEST
VMEM_LIMIT = 16 * 2**20
MIDDLE = 64


def full_dot(a, b, contract):
    return lax.dot_general(
        a, b, (contract, ((), ())), precision=HIGHEST, preferred_element_type=jnp.float32
    )


def spread(x):
    return jnp.broadcast_to(x, (8, 128))


def eliminate(left, right, col, row_ref):
    slot = col // 8 % 4 * 16
    row_ref[slot : slot + 8, :] = left[0]
    row_ref[slot + 8 : slot + 16, :] = right[0]
    rows_left = [row_ref[pl.ds(slot + i, 8, stride=0), :] for i in range(8)]
    rows_right = [row_ref[pl.ds(slot + 8 + i, 8, stride=0), :] for i in range(8)]
    s = [[spread(rows_left[i][:, col + j : col + j + 1]) if j >= i else None for j in range(8)] for i in range(8)]
    inverse = []
    for j in range(8):
        inverse.append(1.0 / s[j][j])
        for i in range(j + 1, 8):
            factor = s[j][i] * inverse[j]
            for k in range(i, 8):
                s[i][k] = s[i][k] - factor * s[j][k]
            rows_left[i] = rows_left[i] - factor * rows_left[j]
            rows_right[i] = rows_right[i] - factor * rows_right[j]
    row = lax.broadcasted_iota(jnp.int32, (8, 128), 0)
    done_left, done_right, scale = rows_left[0], rows_right[0], inverse[0]
    for i in range(1, 8):
        done_left = jnp.where(row == i, rows_left[i], done_left)
        done_right = jnp.where(row == i, rows_right[i], done_right)
        scale = jnp.where(row == i, inverse[i], scale)
    new_left, new_right = [], []
    for x, y in zip(left[1:], right[1:]):
        c = [spread(x[:, col + j : col + j + 1]) for j in range(8)]
        for j in range(8):
            factor = c[j] * inverse[j]
            for k in range(j + 1, 8):
                c[k] = c[k] - factor * s[j][k]
            x = x - factor * rows_left[j]
            y = y - factor * rows_right[j]
        new_left.append(x)
        new_right.append(y)
    return done_left, done_right, scale, new_left, new_right


def invert_block(a, row_ref):
    rows = lax.broadcasted_iota(jnp.int32, (128, 128), 0)
    cols = lax.broadcasted_iota(jnp.int32, (128, 128), 1)
    v = jnp.where(rows == cols, 1.0, 0.0).astype(jnp.float32)
    out = []
    for m in range(0, 128, MIDDLE):
        left = [a[i : i + 8, :] for i in range(0, MIDDLE, 8)]
        right = [v[i : i + 8, :] for i in range(0, MIDDLE, 8)]
        lefts, rights, scales = [], [], []
        for g in range(MIDDLE // 8):
            done_left, done_right, scale, left, right = eliminate(left, right, m + 8 * g, row_ref)
            lefts.append(done_left)
            rights.append(done_right)
            scales.append(scale)
        u, w, d = jnp.concatenate(lefts, 0), jnp.concatenate(rights, 0), jnp.concatenate(scales, 0)
        out.append(w * jnp.sqrt(d))
        if m + MIDDLE < 128:
            factors = (u * d)[:, m + MIDDLE :]
            a = a[MIDDLE:] - full_dot(factors, u, ((0,), (0,)))
            v = v[MIDDLE:] - full_dot(factors, w, ((0,), (0,)))
    return jnp.concatenate(out, 0)


IN_VMEM = pl.BlockSpec(memory_space=pltpu.VMEM)
IN_SMEM = pl.BlockSpec(memory_space=pltpu.SMEM)
ANYWHERE = pl.BlockSpec(memory_space=pl.ANY)


def on_chip(kernel, outputs, scratch, flops, name):
    def call(where, *operands, after=()):
        return pl.pallas_call(
            kernel,
            out_shape=outputs,
            in_specs=[IN_SMEM] + [IN_VMEM] * len(operands) + [ANYWHERE] * len(after),
            out_specs=[IN_VMEM] * len(outputs),
            scratch_shapes=scratch,
            compiler_params=pltpu.CompilerParams(vmem_limit_bytes=VMEM_LIMIT),
            cost_estimate=pl.CostEstimate(flops=flops, bytes_accessed=2**20, transcendentals=0),
            name=name,
        )(where, *operands, *after)

    return call


def pass_kernel(*refs):
    pass


def together(arrays, after):
    n = len(arrays)
    return pl.pallas_call(
        pass_kernel,
        out_shape=[jax.ShapeDtypeStruct(x.shape, x.dtype) for x in arrays],
        in_specs=[ANYWHERE] * (n + 1),
        out_specs=[ANYWHERE] * n,
        input_output_aliases={i: i for i in range(n)},
        name="together",
    )(*arrays, after)


def hold_kernel(where_ref, x_ref, out_ref, top_ref):
    out_ref[...] = x_ref[...]
    top_ref[...] = x_ref[: top_ref.shape[0], :]


def hold(where, x):
    outputs = [array(x.shape, x.dtype), array((x.shape[0] // 2, x.shape[1]), x.dtype)]
    return on_chip(hold_kernel, outputs, [], 10**9, "hold")(where, x)


def array(shape, dtype=jnp.float32):
    return jax.ShapeDtypeStruct(shape, dtype)


GRAY = (0, 1, 3, 2)


def gray(step):
    return step ^ lax.shift_right_logical(step, 1)


def behind(outer, inner, a, m):
    return (outer ^ a) * 4 + lax.rem(inner + 4 - GRAY[m], 4)


def rows_of(block, width):
    return pl.ds(pl.multiple_of(block * width, 8), width)


def load_gram(where_ref, mine_ref, other_ref, a_ref):
    core = where_ref[4]
    blocks, half = mine_ref.shape[:2]
    for i in range(blocks):
        a_ref[rows_of(2 * i + core, half), :] = mine_ref[i]
        a_ref[rows_of(2 * i + 1 - core, half), :] = other_ref[i]


def factor(w_ref, a_ref, row_ref):
    n = w_ref.shape[0]
    w_ref[...] = jnp.zeros_like(w_ref)
    for k in range(0, n, 128):
        block = slice(k, k + 128)
        w = invert_block(a_ref[block, block], row_ref)
        if k:
            w_ref[block, :k] = full_dot(w, w_ref[block, :k], ((1,), (0,)))
        w_ref[block, block] = w
        if k + 128 < n:
            u = full_dot(w, a_ref[block, k + 128 :], ((1,), (0,)))
            a_ref[k + 128 :, k + 128 :] -= full_dot(u, u, ((0,), (0,)))
            w_ref[k + 128 :, : k + 128] -= full_dot(u, w_ref[block, : k + 128], ((0,), (0,)))


def last_basis_kernel(where_ref, mine_ref, other_ref, image_ref, out_ref, w_ref, a_ref, row_ref):
    load_gram(where_ref, mine_ref, other_ref, a_ref)
    factor(w_ref, a_ref, row_ref)
    width = out_ref.shape[0]
    mine = w_ref[rows_of(where_ref[2] * 4 + where_ref[3], width), :]
    out_ref[...] = full_dot(mine, image_ref[...], ((1,), (0,))).astype(out_ref.dtype)


def last_basis(where, mine, other, image):
    n = mine.shape[2]
    square = pltpu.VMEM((n, n), jnp.float32)
    outputs = [array((2 * mine.shape[1], image.shape[1]), jnp.bfloat16)]
    scratch = [square, square, pltpu.VMEM((64, 128), jnp.float32)]
    return on_chip(last_basis_kernel, outputs, scratch, 200 * n**3, "last_basis")(where, mine, other, image)[0]


def put_in_order(where_ref, pieces, block_ref):
    width = pieces[0].shape[1]
    for m, piece in enumerate(pieces):
        for a in range(2):
            block_ref[rows_of(behind(where_ref[2], where_ref[3], a, m), width), :] = piece[a]


def gram_rows(where_ref, block_ref, part_ref, keep_ref, give_ref):
    half = keep_ref.shape[0]
    core = where_ref[4]
    mine = block_ref[rows_of(where_ref[2] * 4 + where_ref[3], 2 * half), :]
    part_ref[...] = full_dot(mine, block_ref[...], ((1,), (1,)))
    keep_ref[...] = part_ref[rows_of(core, half), :]
    give_ref[...] = part_ref[rows_of(1 - core, half), :]


def gram_kernel(where_ref, *refs):
    keep_ref, give_ref, block_ref, part_ref = refs[4:]
    put_in_order(where_ref, refs[:4], block_ref)
    gram_rows(where_ref, block_ref, part_ref, keep_ref, give_ref)


def gram_terms(where, pieces):
    width, features = pieces[0].shape[1:]
    n = 8 * width
    outputs = [array((width // 2, n))] * 2
    scratch = [pltpu.VMEM((n, features), jnp.float32), pltpu.VMEM((width, n), jnp.float32)]
    return on_chip(gram_kernel, outputs, scratch, 2 * 10**9, "gram_terms")(where, *pieces)


def add_kernel(where_ref, *refs):
    pieces, out_ref, terms_ref = refs[:4], refs[4], refs[5]
    for m, piece in enumerate(pieces):
        for a in range(2):
            terms_ref[behind(where_ref[0], where_ref[1], a, m)] = piece[a]
    total = sum(terms_ref[i] for i in range(8))
    for i in range(8):
        out_ref[i] = total


def add_in_order(where, pieces):
    outputs = [array((8,) + pieces[0].shape[1:])]
    return on_chip(add_kernel, outputs, [pltpu.VMEM(outputs[0].shape, jnp.float32)], 10**9, "add_in_order")(
        where, *pieces
    )[0]


def add_both_kernel(scale, where_ref, x_ref, out_ref):
    total = sum(x_ref[i] for i in range(8))
    width = total.shape[0] // 2
    for i in range(8):
        out_ref[i, :width] = total[:width] * scale
        out_ref[i, width:] = total[width:]


def add_both(where, x, scale):
    kernel = functools.partial(add_both_kernel, scale)
    return on_chip(kernel, [array(x.shape)], [], 10**9, "add_both")(where, x)[0]


def normalised_kernel(where_ref, mine_ref, other_ref, image_ref, keep_ref, give_ref, product_ref, w_ref, a_ref, row_ref, part_ref):
    blocks, width, features = mine_ref.shape
    width //= 2
    half = width // 2
    core = where_ref[4]
    for i in range(blocks):
        product_ref[rows_of(i, width), :] = mine_ref[i, :width]
        for j in range(2):
            at = slice(width + j * half, width + (j + 1) * half)
            columns = slice(j * features, (j + 1) * features)
            a_ref[rows_of(2 * i + core, half), columns] = mine_ref[i, at]
            a_ref[rows_of(2 * i + 1 - core, half), columns] = other_ref[i, at]
    factor(w_ref, a_ref, row_ref)
    image_ref[...] = full_dot(w_ref[...], product_ref[...], ((1,), (0,)))
    gram_rows(where_ref, image_ref, part_ref, keep_ref, give_ref)


def normalised(where, mine, other):
    _, width, features = mine.shape
    width //= 2
    n = 8 * width
    outputs = [array((n, features)), array((width // 2, n)), array((width // 2, n))]
    square = pltpu.VMEM((n, n), jnp.float32)
    scratch = [pltpu.VMEM((n, features), jnp.float32), square, square, pltpu.VMEM((64, 128), jnp.float32)]
    scratch += [pltpu.VMEM((width, n), jnp.float32)]
    return on_chip(normalised_kernel, outputs, scratch, 200 * n**3, "normalised")(where, mine, other)


PIECES = [(0, 0, 2), (1, 0, 2), (2, 0, 2), (3, 0, 2), (4, 0, 2), (5, 0, 2), (6, 0, 2), (7, 0, 1), (7, 1, 1)]
BLOCKS = 8


def three_parts(x):
    high = x.astype(jnp.bfloat16)
    rest = x - high.astype(jnp.float32)
    middle = rest.astype(jnp.bfloat16)
    low = (rest - middle.astype(jnp.float32)).astype(jnp.bfloat16)
    return jnp.concatenate([high, middle, low], 0)


def add_parts(total, width):
    return total[:width] + total[width : 2 * width] + total[2 * width :]


def weights(x):
    return (three_parts(x) if x.dtype == jnp.float32 else x).T


def multiply(pieces, weights_ref, store, rows, width):
    tile = rows // 4
    for quarter in range(4):
        total = 0.0
        for piece, (k, first, count) in zip(pieces, PIECES):
            start = quarter * tile - first * rows // 2
            if 0 <= start < count * rows // 2:
                total += jnp.dot(piece[start : start + tile, :], weights_ref[k], preferred_element_type=jnp.float32)
        total = total.T
        store(slice(quarter * tile, (quarter + 1) * tile), add_parts(total, width) if len(total) > width else total)


def first_kernel(where_ref, basis_ref, *refs):
    pieces, out_ref, weights_ref = refs[:-2], refs[-2], refs[-1]
    for a in range(2):
        for m in range(4):
            weights_ref[4 * a + m] = weights(basis_ref[behind(where_ref[2], where_ref[3], a, m)])
    width, rows = out_ref.shape

    def store(at, value):
        out_ref[:, at] = value

    multiply(pieces, weights_ref, store, rows, width)


def load_from_rows(where_ref, basis, weights_ref):
    for m in range(4):
        for a in range(2):
            block = behind(where_ref[0], where_ref[1], a, m)
            step = lax.rem(where_ref[3] + 4 - lax.rem(block, 4), 4)
            place = (lax.div(block, 4) ^ where_ref[2]) * 4 + gray(step)
            weights_ref[place] = weights(basis[m][a])


def next_kernel(where_ref, *refs):
    pieces, out_ref, weights_ref = refs[4:-2], refs[-2], refs[-1]
    load_from_rows(where_ref, refs[:4], weights_ref)
    width, rows = out_ref.shape

    def store(at, value):
        out_ref[:, at] = value

    multiply(pieces, weights_ref, store, rows, width)


def compressed_kernel(where_ref, *refs):
    pieces, (keep_ref, give_ref, weights_ref, out_ref) = refs[4:-4], refs[-4:]
    load_from_rows(where_ref, refs[:4], weights_ref)
    width, rows = out_ref.shape
    half = width // 2
    core = where_ref[4]

    def store(at, value):
        out_ref[:, at] = value

    multiply(pieces, weights_ref, store, rows, width)
    keep_ref[...] = out_ref[rows_of(core, half), :]
    give_ref[...] = out_ref[rows_of(1 - core, half), :]


def product_flops(rows, width, features):
    return 16 * rows * width * BLOCKS * features


def first_product(where, basis, pieces):
    width, features = basis.shape[1:]
    rows = pieces[0].shape[0]
    scratch = [pltpu.VMEM((BLOCKS, features, 3 * width), jnp.bfloat16)]
    return on_chip(first_kernel, [array((width, rows))], scratch, product_flops(rows, width, features), "first_product")(
        where, basis, *pieces
    )[0]


def next_product(where, basis, pieces):
    width, features = basis[0].shape[1:]
    rows = pieces[0].shape[0]
    scratch = [pltpu.VMEM((BLOCKS, features, 3 * width), jnp.bfloat16)]
    return on_chip(next_kernel, [array((width, rows))], scratch, product_flops(rows, width, features), "next_product")(
        where, *basis, *pieces
    )[0]


def compress(where, basis, pieces):
    width, features = basis[0].shape[1:]
    rows = pieces[0].shape[0]
    outputs = [array((width // 2, rows))] * 2
    scratch = [pltpu.VMEM((BLOCKS, features, width), jnp.bfloat16), pltpu.VMEM((width, rows), jnp.float32)]
    return on_chip(compressed_kernel, outputs, scratch, product_flops(rows, width, features), "compress")(
        where, *basis, *pieces
    )


def back_kernel(where_ref, mine_ref, other_ref, *refs):
    pieces, outs, (sums_ref, parts_ref) = refs[:-6], refs[-6:-2], refs[-2:]
    width, rows = mine_ref.shape
    parts_ref[...] = three_parts(mine_ref[...] + other_ref[...])
    for block in range(BLOCKS):
        total = 0.0
        for piece, (k, first, count) in zip(pieces, PIECES):
            if k == block:
                at = slice(first * rows // 2, (first + count) * rows // 2)
                total += jnp.dot(parts_ref[:, at], piece[...], preferred_element_type=jnp.float32)
        target = behind(where_ref[2], where_ref[3], block // 4, block % 4)
        step = lax.rem(lax.rem(target, 4) + 4 - where_ref[1], 4)
        sums_ref[gray(step) * 2 + (lax.div(target, 4) ^ where_ref[0])] = add_parts(total, width)
    for m in range(4):
        outs[m][...] = sums_ref[2 * m : 2 * m + 2]


def back_and_gram_kernel(where_ref, mine_ref, other_ref, keep_ref, got_ref, *refs):
    pieces, (out_ref, parts_ref) = refs[:-2], refs[-2:]
    width, rows = mine_ref.shape
    features = out_ref.shape[2]
    gram = keep_ref[...] + got_ref[...]
    half = gram.shape[0]
    for i in range(BLOCKS):
        for j in range(2):
            out_ref[i, width + j * half : width + (j + 1) * half] = gram[:, j * features : (j + 1) * features]
    parts_ref[...] = three_parts(mine_ref[...] + other_ref[...])
    for block in range(BLOCKS):
        total = 0.0
        for piece, (k, first, count) in zip(pieces, PIECES):
            if k == block:
                at = slice(first * rows // 2, (first + count) * rows // 2)
                total += jnp.dot(parts_ref[:, at], piece[...], preferred_element_type=jnp.float32)
        target = behind(where_ref[2], where_ref[3], block // 4, block % 4)
        out_ref[target, :width] = add_parts(total, width)


def back_and_gram(where, mine, other, keep, got, pieces):
    width, rows = mine.shape
    features = pieces[0].shape[1]
    outputs = [array((BLOCKS, 2 * width, features))]
    scratch = [pltpu.VMEM((3 * width, rows), jnp.bfloat16)]
    return on_chip(back_and_gram_kernel, outputs, scratch, product_flops(rows, width, features), "back_and_gram")(
        where, mine, other, keep, got, *pieces
    )[0]


def back_product(where, mine, other, pieces):
    width, rows = mine.shape
    features = pieces[0].shape[1]
    outputs = [array((2, width, features))] * 4
    scratch = [pltpu.VMEM((BLOCKS, width, features), jnp.float32), pltpu.VMEM((3 * width, rows), jnp.bfloat16)]
    return on_chip(back_kernel, outputs, scratch, product_flops(rows, width, features), "back_product")(
        where, mine, other, *pieces
    )


def exchange(x, axes):
    return lax.all_to_all(x, axes, 0, 0, tiled=True)


def swap(x, axis):
    return lax.ppermute(x, axis, [(0, 1), (1, 0)])


def shift(x, axis, step):
    return lax.ppermute(x, axis, [(i, (i + step) % 4) for i in range(4)])


def fan_out(x, axes):
    outer, inner = axes
    pair = jnp.stack([x, swap(x, outer)])
    return [pair] + [shift(pair, inner, GRAY[m]) for m in (1, 2, 3)]


def fan_in(pairs, axes):
    outer, inner = axes
    pair = pairs[0] + sum(shift(pairs[m], inner, GRAY[m]) for m in (1, 2, 3))
    return pair[0] + swap(pair[1], outer)


def gather_entities(where, x, basis):
    half = x.shape[0] // 2
    before, after = shift(x, "z", 1), shift(x, "z", 3)
    across = swap(x, "y_lo")
    before, after, across = together([before, after, across], basis)
    far = shift(before, "z", 1)
    across_before = swap(before, "y_lo")
    across_after = shift(across, "z", 3)
    far, far_half = hold(where, far)
    far_top = swap(far_half, "y_lo")
    far_low = shift(across_after[half:], "z", 3)
    return [hold(where, x)[0], before, after, far, across, across_before, across_after, far_top, far_low]


def whole_gram(where, part):
    part = exchange(add_in_order(where, fan_out(part, ROWS)), PLANE)
    return part, swap(part, "core")


def local(entities, start_basis):
    rows, features = entities.shape
    total_rows = rows * lax.axis_size(ROWS)
    width = start_basis.shape[1] // 8
    where = jnp.stack([lax.axis_index(a) for a in ROWS + COLS]).astype(jnp.int32)

    basis = exchange(start_basis.T.reshape(8, width, features), PLANE)
    pieces = gather_entities(where, entities, basis)

    image = first_product(where, basis, pieces)
    image = fan_in(back_product(where, image, swap(image, "core"), pieces), ROWS) / total_rows
    keep, give = gram_terms(where, fan_out(image, PLANE))
    for step in range(1, ITERS):
        product = next_product(where, fan_out(image, ROWS), pieces)
        sent = back_and_gram(where, product, swap(product, "core"), keep, swap(give, "core"), pieces)
        both = exchange(add_both(where, exchange(sent, ROWS), 1.0 / total_rows), PLANE)
        block, keep, give = normalised(where, both, swap(both, "core"))
    part = keep + swap(give, "core")
    rounded = last_basis(where, *whole_gram(where, part), block)
    keep, give = compress(where, fan_out(rounded, ROWS), pieces)
    return (keep + swap(give, "core")).T.astype(jnp.bfloat16)


def solution(mesh):
    fine = Mesh(mesh.devices.reshape(2, 4, 2, 4, 2), ROWS + COLS)
    return jax.shard_map(
        local,
        mesh=fine,
        in_specs=(P(ROWS, COLS), P(COLS, None)),
        out_specs=P(ROWS, COLS),
        check_vma=False,
    )
```

```python
import functools

import jax
import jax.numpy as jnp
from jax import lax
from jax.experimental import pallas as pl
from jax.experimental.pallas import tpu as pltpu
from jax.sharding import Mesh, PartitionSpec as P

ITERS = 2
ROWS = ("y_hi", "x")
PLANE = ("y_lo", "z")
COLS = ("y_lo", "z", "core")
HIGHEST = lax.Precision.HIGHEST
VMEM_LIMIT = 16 * 2**20
MIDDLE = 64


def full_dot(a, b, contract):
    return lax.dot_general(
        a, b, (contract, ((), ())), precision=HIGHEST, preferred_element_type=jnp.float32
    )


def spread(x):
    return jnp.broadcast_to(x, (8, 128))


def eliminate(left, right, col, row_ref):
    slot = col // 8 % 4 * 16
    row_ref[slot : slot + 8, :] = left[0]
    row_ref[slot + 8 : slot + 16, :] = right[0]
    rows_left = [row_ref[pl.ds(slot + i, 8, stride=0), :] for i in range(8)]
    rows_right = [row_ref[pl.ds(slot + 8 + i, 8, stride=0), :] for i in range(8)]
    s = [[spread(rows_left[i][:, col + j : col + j + 1]) if j >= i else None for j in range(8)] for i in range(8)]
    inverse = []
    for j in range(8):
        inverse.append(1.0 / s[j][j])
        for i in range(j + 1, 8):
            factor = s[j][i] * inverse[j]
            for k in range(i, 8):
                s[i][k] = s[i][k] - factor * s[j][k]
            rows_left[i] = rows_left[i] - factor * rows_left[j]
            rows_right[i] = rows_right[i] - factor * rows_right[j]
    row = lax.broadcasted_iota(jnp.int32, (8, 128), 0)
    done_left, done_right, scale = rows_left[0], rows_right[0], inverse[0]
    for i in range(1, 8):
        done_left = jnp.where(row == i, rows_left[i], done_left)
        done_right = jnp.where(row == i, rows_right[i], done_right)
        scale = jnp.where(row == i, inverse[i], scale)
    new_left, new_right = [], []
    for x, y in zip(left[1:], right[1:]):
        c = [spread(x[:, col + j : col + j + 1]) for j in range(8)]
        for j in range(8):
            factor = c[j] * inverse[j]
            for k in range(j + 1, 8):
                c[k] = c[k] - factor * s[j][k]
            x = x - factor * rows_left[j]
            y = y - factor * rows_right[j]
        new_left.append(x)
        new_right.append(y)
    return done_left, done_right, scale, new_left, new_right


def invert_block(a, row_ref):
    rows = lax.broadcasted_iota(jnp.int32, (128, 128), 0)
    cols = lax.broadcasted_iota(jnp.int32, (128, 128), 1)
    v = jnp.where(rows == cols, 1.0, 0.0).astype(jnp.float32)
    out = []
    for m in range(0, 128, MIDDLE):
        left = [a[i : i + 8, :] for i in range(0, MIDDLE, 8)]
        right = [v[i : i + 8, :] for i in range(0, MIDDLE, 8)]
        lefts, rights, scales = [], [], []
        for g in range(MIDDLE // 8):
            done_left, done_right, scale, left, right = eliminate(left, right, m + 8 * g, row_ref)
            lefts.append(done_left)
            rights.append(done_right)
            scales.append(scale)
        u, w, d = jnp.concatenate(lefts, 0), jnp.concatenate(rights, 0), jnp.concatenate(scales, 0)
        out.append(w * jnp.sqrt(d))
        if m + MIDDLE < 128:
            factors = (u * d)[:, m + MIDDLE :]
            a = a[MIDDLE:] - full_dot(factors, u, ((0,), (0,)))
            v = v[MIDDLE:] - full_dot(factors, w, ((0,), (0,)))
    return jnp.concatenate(out, 0)


IN_VMEM = pl.BlockSpec(memory_space=pltpu.VMEM)
IN_SMEM = pl.BlockSpec(memory_space=pltpu.SMEM)
ANYWHERE = pl.BlockSpec(memory_space=pl.ANY)


def on_chip(kernel, outputs, scratch, flops, name):
    def call(where, *operands, after=()):
        return pl.pallas_call(
            kernel,
            out_shape=outputs,
            in_specs=[IN_SMEM] + [IN_VMEM] * len(operands) + [ANYWHERE] * len(after),
            out_specs=[IN_VMEM] * len(outputs),
            scratch_shapes=scratch,
            compiler_params=pltpu.CompilerParams(vmem_limit_bytes=VMEM_LIMIT),
            cost_estimate=pl.CostEstimate(flops=flops, bytes_accessed=2**20, transcendentals=0),
            name=name,
        )(where, *operands, *after)

    return call


def hold_kernel(where_ref, x_ref, *refs):
    out_ref, top_ref = refs[-2:]
    out_ref[...] = x_ref[...]
    top_ref[...] = x_ref[: top_ref.shape[0], :]


def hold(where, x, after=()):
    outputs = [array(x.shape, x.dtype), array((x.shape[0] // 2, x.shape[1]), x.dtype)]
    return on_chip(hold_kernel, outputs, [], 10**9, "hold")(where, x, after=after)


def array(shape, dtype=jnp.float32):
    return jax.ShapeDtypeStruct(shape, dtype)


GRAY = (0, 1, 3, 2)


def gray(step):
    return step ^ lax.shift_right_logical(step, 1)


def behind(outer, inner, a, m):
    return (outer ^ a) * 4 + lax.rem(inner + 4 - GRAY[m], 4)


def rows_of(block, width):
    return pl.ds(pl.multiple_of(block * width, 8), width)


def load_gram(where_ref, mine_ref, other_ref, a_ref):
    core = where_ref[4]
    blocks, half = mine_ref.shape[:2]
    for i in range(blocks):
        a_ref[rows_of(2 * i + core, half), :] = mine_ref[i]
        a_ref[rows_of(2 * i + 1 - core, half), :] = other_ref[i]


def factor(w_ref, a_ref, row_ref):
    n = w_ref.shape[0]
    w_ref[...] = jnp.zeros_like(w_ref)
    for k in range(0, n, 128):
        block = slice(k, k + 128)
        w = invert_block(a_ref[block, block], row_ref)
        if k:
            w_ref[block, :k] = full_dot(w, w_ref[block, :k], ((1,), (0,)))
        w_ref[block, block] = w
        if k + 128 < n:
            u = full_dot(w, a_ref[block, k + 128 :], ((1,), (0,)))
            for r in range(k + 128, n, 128):
                below, right = u[:, r - k - 128 : r - k], u[:, r - k - 128 :]
                a_ref[r : r + 128, r:] -= full_dot(below, right, ((0,), (0,)))
            w_ref[k + 128 :, : k + 128] -= full_dot(u, w_ref[block, : k + 128], ((0,), (0,)))


def last_basis_kernel(where_ref, mine_ref, other_ref, image_ref, out_ref, w_ref, a_ref, row_ref):
    load_gram(where_ref, mine_ref, other_ref, a_ref)
    factor(w_ref, a_ref, row_ref)
    width = out_ref.shape[0]
    mine = w_ref[rows_of(where_ref[2] * 4 + where_ref[3], width), :]
    out_ref[...] = full_dot(mine, image_ref[...], ((1,), (0,))).astype(out_ref.dtype)


def last_basis(where, mine, other, image):
    n = mine.shape[2]
    square = pltpu.VMEM((n, n), jnp.float32)
    outputs = [array((2 * mine.shape[1], image.shape[1]), jnp.bfloat16)]
    scratch = [square, square, pltpu.VMEM((64, 128), jnp.float32)]
    return on_chip(last_basis_kernel, outputs, scratch, 200 * n**3, "last_basis")(where, mine, other, image)[0]


def put_in_order(where_ref, pieces, block_ref):
    width = pieces[0].shape[1]
    for m, piece in enumerate(pieces):
        for a in range(2):
            block_ref[rows_of(behind(where_ref[2], where_ref[3], a, m), width), :] = piece[a]


def gram_rows(where_ref, block_ref, part_ref, keep_ref, give_ref):
    half = keep_ref.shape[0]
    core = where_ref[4]
    mine = block_ref[rows_of(where_ref[2] * 4 + where_ref[3], 2 * half), :]
    part_ref[...] = full_dot(mine, block_ref[...], ((1,), (1,)))
    keep_ref[...] = part_ref[rows_of(core, half), :]
    give_ref[...] = part_ref[rows_of(1 - core, half), :]


def gram_kernel(where_ref, *refs):
    keep_ref, give_ref, block_ref, part_ref = refs[4:]
    put_in_order(where_ref, refs[:4], block_ref)
    gram_rows(where_ref, block_ref, part_ref, keep_ref, give_ref)


def gram_terms(where, pieces):
    width, features = pieces[0].shape[1:]
    n = 8 * width
    outputs = [array((width // 2, n))] * 2
    scratch = [pltpu.VMEM((n, features), jnp.float32), pltpu.VMEM((width, n), jnp.float32)]
    return on_chip(gram_kernel, outputs, scratch, 2 * 10**9, "gram_terms")(where, *pieces)


def add_kernel(where_ref, *refs):
    pieces, out_ref, terms_ref = refs[:4], refs[4], refs[5]
    for m, piece in enumerate(pieces):
        for a in range(2):
            terms_ref[behind(where_ref[0], where_ref[1], a, m)] = piece[a]
    total = sum(terms_ref[i] for i in range(8))
    for i in range(8):
        out_ref[i] = total


def add_in_order(where, pieces):
    outputs = [array((8,) + pieces[0].shape[1:])]
    return on_chip(add_kernel, outputs, [pltpu.VMEM(outputs[0].shape, jnp.float32)], 10**9, "add_in_order")(
        where, *pieces
    )[0]


def add_both_kernel(scale, where_ref, x_ref, out_ref):
    total = sum(x_ref[i] for i in range(8))
    width = total.shape[0] // 2
    for i in range(8):
        out_ref[i, :width] = total[:width] * scale
        out_ref[i, width:] = total[width:]


def add_both(where, x, scale):
    kernel = functools.partial(add_both_kernel, scale)
    return on_chip(kernel, [array(x.shape)], [], 10**9, "add_both")(where, x)[0]


def normalised_kernel(where_ref, mine_ref, other_ref, image_ref, keep_ref, give_ref, product_ref, w_ref, a_ref, row_ref, part_ref):
    blocks, width, features = mine_ref.shape
    width //= 2
    half = width // 2
    core = where_ref[4]
    for i in range(blocks):
        product_ref[rows_of(i, width), :] = mine_ref[i, :width]
        for j in range(2):
            at = slice(width + j * half, width + (j + 1) * half)
            columns = slice(j * features, (j + 1) * features)
            a_ref[rows_of(2 * i + core, half), columns] = mine_ref[i, at]
            a_ref[rows_of(2 * i + 1 - core, half), columns] = other_ref[i, at]
    factor(w_ref, a_ref, row_ref)
    image_ref[...] = full_dot(w_ref[...], product_ref[...], ((1,), (0,)))
    gram_rows(where_ref, image_ref, part_ref, keep_ref, give_ref)


def normalised(where, mine, other):
    _, width, features = mine.shape
    width //= 2
    n = 8 * width
    outputs = [array((n, features)), array((width // 2, n)), array((width // 2, n))]
    square = pltpu.VMEM((n, n), jnp.float32)
    scratch = [pltpu.VMEM((n, features), jnp.float32), square, square, pltpu.VMEM((64, 128), jnp.float32)]
    scratch += [pltpu.VMEM((width, n), jnp.float32)]
    return on_chip(normalised_kernel, outputs, scratch, 200 * n**3, "normalised")(where, mine, other)


PIECES = [(0, 0, 2), (1, 0, 2), (2, 0, 2), (3, 0, 2), (4, 0, 2), (5, 0, 2), (6, 0, 2), (7, 0, 1), (7, 1, 1)]
BLOCKS = 8


def three_parts(x):
    high = x.astype(jnp.bfloat16)
    rest = x - high.astype(jnp.float32)
    middle = rest.astype(jnp.bfloat16)
    low = (rest - middle.astype(jnp.float32)).astype(jnp.bfloat16)
    return jnp.concatenate([high, middle, low], 0)


def add_parts(total, width):
    return total[:width] + total[width : 2 * width] + total[2 * width :]


def weights(x):
    return (three_parts(x) if x.dtype == jnp.float32 else x).T


def multiply(pieces, weights_ref, out_ref, blocks=range(8), start_ref=None):
    width, rows = out_ref.shape
    tile = rows // 4
    for quarter in range(4):
        total = 0.0
        for piece, (k, first, count) in zip(pieces, [p for p in PIECES if p[0] in blocks]):
            start = quarter * tile - first * rows // 2
            if 0 <= start < count * rows // 2:
                total += jnp.dot(piece[start : start + tile, :], weights_ref[k], preferred_element_type=jnp.float32)
        total = total.T
        at = slice(quarter * tile, (quarter + 1) * tile)
        total = add_parts(total, width) if len(total) > width else total
        out_ref[:, at] = total if start_ref is None else start_ref[:, at] + total


def first_kernel(blocks, where_ref, *refs):
    basis, pieces, (out_ref, weights_ref, block_ref) = refs[:4], refs[4:-3], refs[-3:]
    for k in blocks:
        block = behind(where_ref[2], where_ref[3], k // 4, k % 4)
        for m in range(4):
            part = basis[m][block]
            block_ref[rows_of(behind(0, where_ref[1], 0, m), part.shape[0]), :] = part
        weights_ref[k] = weights(block_ref[...])
    if blocks[0] == 0:
        multiply(pieces, weights_ref, out_ref, blocks)
    else:
        multiply(pieces[1:], weights_ref, out_ref, blocks, pieces[0])


def load_from_rows(where_ref, basis, weights_ref):
    for m in range(4):
        for a in range(2):
            block = behind(where_ref[0], where_ref[1], a, m)
            step = lax.rem(where_ref[3] + 4 - lax.rem(block, 4), 4)
            place = (lax.div(block, 4) ^ where_ref[2]) * 4 + gray(step)
            weights_ref[place] = weights(basis[m][a])


def next_kernel(where_ref, *refs):
    pieces, out_ref, weights_ref = refs[4 : 4 + len(PIECES)], refs[-2], refs[-1]
    load_from_rows(where_ref, refs[:4], weights_ref)
    multiply(pieces, weights_ref, out_ref)


def compressed_kernel(where_ref, *refs):
    pieces, (keep_ref, give_ref, weights_ref, out_ref) = refs[4:-4], refs[-4:]
    load_from_rows(where_ref, refs[:4], weights_ref)
    multiply(pieces, weights_ref, out_ref)
    half = keep_ref.shape[0]
    core = where_ref[4]
    keep_ref[...] = out_ref[rows_of(core, half), :]
    give_ref[...] = out_ref[rows_of(1 - core, half), :]


def product_flops(rows, width, features):
    return 16 * rows * width * BLOCKS * features


def first_product(where, basis, pieces):
    features = basis[0].shape[2]
    width = 4 * basis[0].shape[1]
    rows = pieces[0].shape[0]
    scratch = [pltpu.VMEM((BLOCKS, features, 3 * width), jnp.bfloat16), pltpu.VMEM((width, features), jnp.float32)]
    flops = product_flops(rows, width, features)
    outputs = [array((width, rows))]
    early = sum(k < BLOCKS - 1 for k, _, _ in PIECES)
    kernel = functools.partial(first_kernel, range(BLOCKS - 1))
    out = on_chip(kernel, outputs, scratch, flops, "first_product")(where, *basis, *pieces[:early])[0]
    kernel = functools.partial(first_kernel, range(BLOCKS - 1, BLOCKS))
    return on_chip(kernel, outputs, scratch, flops // 8, "first_product_end")(where, *basis, out, *pieces[early:])[0]


def next_product(where, basis, pieces, after):
    width, features = basis[0].shape[1:]
    rows = pieces[0].shape[0]
    scratch = [pltpu.VMEM((BLOCKS, features, 3 * width), jnp.bfloat16)]
    return on_chip(next_kernel, [array((width, rows))], scratch, product_flops(rows, width, features), "next_product")(
        where, *basis, *pieces, after=after
    )[0]


def compress(where, basis, pieces):
    width, features = basis[0].shape[1:]
    rows = pieces[0].shape[0]
    outputs = [array((width // 2, rows))] * 2
    scratch = [pltpu.VMEM((BLOCKS, features, width), jnp.bfloat16), pltpu.VMEM((width, rows), jnp.float32)]
    return on_chip(compressed_kernel, outputs, scratch, product_flops(rows, width, features), "compress")(
        where, *basis, *pieces
    )


def back_kernel(where_ref, mine_ref, other_ref, *refs):
    pieces, outs, (sums_ref, parts_ref) = refs[:-6], refs[-6:-2], refs[-2:]
    width, rows = mine_ref.shape
    parts_ref[...] = three_parts(mine_ref[...] + other_ref[...])
    for block in range(BLOCKS):
        total = 0.0
        for piece, (k, first, count) in zip(pieces, PIECES):
            if k == block:
                at = slice(first * rows // 2, (first + count) * rows // 2)
                total += jnp.dot(parts_ref[:, at], piece[...], preferred_element_type=jnp.float32)
        target = behind(where_ref[2], where_ref[3], block // 4, block % 4)
        step = lax.rem(lax.rem(target, 4) + 4 - where_ref[1], 4)
        sums_ref[gray(step) * 2 + (lax.div(target, 4) ^ where_ref[0])] = add_parts(total, width)
    for m in range(4):
        outs[m][...] = sums_ref[2 * m : 2 * m + 2]


def back_and_gram_kernel(where_ref, mine_ref, other_ref, keep_ref, got_ref, *refs):
    pieces, (out_ref, parts_ref) = refs[:-2], refs[-2:]
    width, rows = mine_ref.shape
    features = out_ref.shape[2]
    gram = keep_ref[...] + got_ref[...]
    half = gram.shape[0]
    for i in range(BLOCKS):
        for j in range(2):
            out_ref[i, width + j * half : width + (j + 1) * half] = gram[:, j * features : (j + 1) * features]
    parts_ref[...] = three_parts(mine_ref[...] + other_ref[...])
    for block in range(BLOCKS):
        total = 0.0
        for piece, (k, first, count) in zip(pieces, PIECES):
            if k == block:
                at = slice(first * rows // 2, (first + count) * rows // 2)
                total += jnp.dot(parts_ref[:, at], piece[...], preferred_element_type=jnp.float32)
        target = behind(where_ref[2], where_ref[3], block // 4, block % 4)
        out_ref[target, :width] = add_parts(total, width)


def back_and_gram(where, mine, other, keep, got, pieces):
    width, rows = mine.shape
    features = pieces[0].shape[1]
    outputs = [array((BLOCKS, 2 * width, features))]
    scratch = [pltpu.VMEM((3 * width, rows), jnp.bfloat16)]
    return on_chip(back_and_gram_kernel, outputs, scratch, product_flops(rows, width, features), "back_and_gram")(
        where, mine, other, keep, got, *pieces
    )[0]


def back_product(where, mine, other, pieces):
    width, rows = mine.shape
    features = pieces[0].shape[1]
    outputs = [array((2, width, features))] * 4
    scratch = [pltpu.VMEM((BLOCKS, width, features), jnp.float32), pltpu.VMEM((3 * width, rows), jnp.bfloat16)]
    return on_chip(back_kernel, outputs, scratch, product_flops(rows, width, features), "back_product")(
        where, mine, other, *pieces
    )


def exchange(x, axes):
    return lax.all_to_all(x, axes, 0, 0, tiled=True)


def swap(x, axis):
    return lax.ppermute(x, axis, [(0, 1), (1, 0)])


def shift(x, axis, step):
    return lax.ppermute(x, axis, [(i, (i + step) % 4) for i in range(4)])


def fan_out(x, axes):
    outer, inner = axes
    pair = jnp.stack([x, swap(x, outer)])
    return [pair] + [shift(pair, inner, GRAY[m]) for m in (1, 2, 3)]


def fan_in(pairs, axes):
    outer, inner = axes
    pair = pairs[0] + sum(shift(pairs[m], inner, GRAY[m]) for m in (1, 2, 3))
    return pair[0] + swap(pair[1], outer)


def gather_all(where, x, start_basis):
    features, n = start_basis.shape
    mine = lax.dynamic_index_in_dim(start_basis.reshape(features, 8, 4, n // 32), where[1], 2, False)
    basis = exchange(mine.transpose(1, 2, 0), PLANE)
    half = x.shape[0] // 2
    before, after = shift(x, "z", 1), shift(x, "z", 3)
    across = swap(x, "y_lo")
    before, _ = hold(where, before, (after, basis))
    basis = [basis] + [shift(basis, "x", GRAY[m]) for m in (1, 2, 3)]
    far = shift(before, "z", 1)
    across_before = swap(before, "y_lo")
    across_after = shift(across, "z", 3)
    far, far_half = hold(where, far, (basis[1], basis[2], basis[3]))
    far_top = swap(far_half, "y_lo")
    far_low = shift(across_after[half:], "z", 3)
    return [hold(where, x)[0], before, after, far, across, across_before, across_after, far_top, far_low], basis


def whole_gram(where, part):
    part = exchange(add_in_order(where, fan_out(part, ROWS)), PLANE)
    return part, swap(part, "core")


def local(entities, start_basis):
    total_rows = entities.shape[0] * lax.axis_size(ROWS)
    where = jnp.stack([lax.axis_index(a) for a in ROWS + COLS]).astype(jnp.int32)

    pieces, basis = gather_all(where, entities, start_basis)

    image = first_product(where, basis, pieces)
    image = fan_in(back_product(where, image, swap(image, "core"), pieces), ROWS) / total_rows
    columns = fan_out(image, PLANE)
    keep, give = gram_terms(where, columns)
    for step in range(1, ITERS):
        product = next_product(where, fan_out(image, ROWS), pieces, columns)
        sent = back_and_gram(where, product, swap(product, "core"), keep, swap(give, "core"), pieces)
        both = exchange(add_both(where, exchange(sent, ROWS), 1.0 / total_rows), PLANE)
        block, keep, give = normalised(where, both, swap(both, "core"))
    part = keep + swap(give, "core")
    rounded = last_basis(where, *whole_gram(where, part), block)
    keep, give = compress(where, fan_out(rounded, ROWS), pieces)
    return (keep + swap(give, "core")).T.astype(jnp.bfloat16)


def solution(mesh):
    fine = Mesh(mesh.devices.reshape(2, 4, 2, 4, 2), ROWS + COLS)
    return jax.shard_map(
        local,
        mesh=fine,
        in_specs=(P(ROWS, COLS), P(COLS, None)),
        out_specs=P(ROWS, COLS),
        check_vma=False,
    )
```

```python
import functools

import jax
import jax.numpy as jnp
from jax import lax
from jax.experimental import pallas as pl
from jax.experimental.pallas import tpu as pltpu
from jax.sharding import Mesh, PartitionSpec as P

ITERS = 2
ROWS = ("y_hi", "x")
PLANE = ("y_lo", "z")
COLS = ("y_lo", "z", "core")
HIGHEST = lax.Precision.HIGHEST
VMEM_LIMIT = 16 * 2**20
MIDDLE = 64


def full_dot(a, b, contract):
    return lax.dot_general(
        a, b, (contract, ((), ())), precision=HIGHEST, preferred_element_type=jnp.float32
    )


def spread(x):
    return jnp.broadcast_to(x, (8, 128))


def eliminate(left, right, col, row_ref):
    slot = col // 8 % 4 * 16
    row_ref[slot : slot + 8, :] = left[0]
    row_ref[slot + 8 : slot + 16, :] = right[0]
    rows_left = [row_ref[pl.ds(slot + i, 8, stride=0), :] for i in range(8)]
    rows_right = [row_ref[pl.ds(slot + 8 + i, 8, stride=0), :] for i in range(8)]
    s = [[spread(rows_left[i][:, col + j : col + j + 1]) if j >= i else None for j in range(8)] for i in range(8)]
    inverse = []
    for j in range(8):
        inverse.append(1.0 / s[j][j])
        for i in range(j + 1, 8):
            factor = s[j][i] * inverse[j]
            for k in range(i, 8):
                s[i][k] = s[i][k] - factor * s[j][k]
            rows_left[i] = rows_left[i] - factor * rows_left[j]
            rows_right[i] = rows_right[i] - factor * rows_right[j]
    row = lax.broadcasted_iota(jnp.int32, (8, 128), 0)
    done_left, done_right, scale = rows_left[0], rows_right[0], inverse[0]
    for i in range(1, 8):
        done_left = jnp.where(row == i, rows_left[i], done_left)
        done_right = jnp.where(row == i, rows_right[i], done_right)
        scale = jnp.where(row == i, inverse[i], scale)
    new_left, new_right = [], []
    for x, y in zip(left[1:], right[1:]):
        c = [spread(x[:, col + j : col + j + 1]) for j in range(8)]
        for j in range(8):
            factor = c[j] * inverse[j]
            for k in range(j + 1, 8):
                c[k] = c[k] - factor * s[j][k]
            x = x - factor * rows_left[j]
            y = y - factor * rows_right[j]
        new_left.append(x)
        new_right.append(y)
    return done_left, done_right, scale, new_left, new_right


def invert_block(a, row_ref):
    rows = lax.broadcasted_iota(jnp.int32, (128, 128), 0)
    cols = lax.broadcasted_iota(jnp.int32, (128, 128), 1)
    v = jnp.where(rows == cols, 1.0, 0.0).astype(jnp.float32)
    out = []
    for m in range(0, 128, MIDDLE):
        left = [a[i : i + 8, :] for i in range(0, MIDDLE, 8)]
        right = [v[i : i + 8, :] for i in range(0, MIDDLE, 8)]
        lefts, rights, scales = [], [], []
        for g in range(MIDDLE // 8):
            done_left, done_right, scale, left, right = eliminate(left, right, m + 8 * g, row_ref)
            lefts.append(done_left)
            rights.append(done_right)
            scales.append(scale)
        u, w, d = jnp.concatenate(lefts, 0), jnp.concatenate(rights, 0), jnp.concatenate(scales, 0)
        out.append(w * jnp.sqrt(d))
        if m + MIDDLE < 128:
            factors = (u * d)[:, m + MIDDLE :]
            a = a[MIDDLE:] - full_dot(factors, u, ((0,), (0,)))
            v = v[MIDDLE:] - full_dot(factors, w, ((0,), (0,)))
    return jnp.concatenate(out, 0)


IN_VMEM = pl.BlockSpec(memory_space=pltpu.VMEM)
IN_SMEM = pl.BlockSpec(memory_space=pltpu.SMEM)
ANYWHERE = pl.BlockSpec(memory_space=pl.ANY)


def on_chip(kernel, outputs, scratch, flops, name):
    def call(where, *operands, after=()):
        return pl.pallas_call(
            kernel,
            out_shape=outputs,
            in_specs=[IN_SMEM] + [IN_VMEM] * len(operands) + [ANYWHERE] * len(after),
            out_specs=[IN_VMEM] * len(outputs),
            scratch_shapes=scratch,
            compiler_params=pltpu.CompilerParams(vmem_limit_bytes=VMEM_LIMIT),
            cost_estimate=pl.CostEstimate(flops=flops, bytes_accessed=2**20, transcendentals=0),
            name=name,
        )(where, *operands, *after)

    return call


def hold_kernel(where_ref, x_ref, *refs):
    out_ref, top_ref = refs[-2:]
    out_ref[...] = x_ref[...]
    top_ref[...] = x_ref[: top_ref.shape[0], :]


def hold(where, x, after=()):
    outputs = [array(x.shape, x.dtype), array((x.shape[0] // 2, x.shape[1]), x.dtype)]
    return on_chip(hold_kernel, outputs, [], 10**9, "hold")(where, x, after=after)


def array(shape, dtype=jnp.float32):
    return jax.ShapeDtypeStruct(shape, dtype)


GRAY = (0, 1, 3, 2)


def gray(step):
    return step ^ lax.shift_right_logical(step, 1)


def behind(outer, inner, a, m):
    return (outer ^ a) * 4 + lax.rem(inner + 4 - GRAY[m], 4)


def rows_of(block, width):
    return pl.ds(pl.multiple_of(block * width, 8), width)


def load_gram(where_ref, mine_ref, other_ref, a_ref):
    core = where_ref[4]
    blocks, half = mine_ref.shape[:2]
    for i in range(blocks):
        a_ref[rows_of(2 * i + core, half), :] = mine_ref[i]
        a_ref[rows_of(2 * i + 1 - core, half), :] = other_ref[i]


def solve(x_ref, a_ref, row_ref):
    n = a_ref.shape[0]
    for k in range(0, n, 128):
        block = slice(k, k + 128)
        w = invert_block(a_ref[block, block], row_ref)
        x = full_dot(w, x_ref[block, :], ((1,), (0,)))
        x_ref[block, :] = x
        if k + 128 < n:
            u = full_dot(w, a_ref[block, k + 128 :], ((1,), (0,)))
            for r in range(k + 128, n, 128):
                below, right = u[:, r - k - 128 : r - k], u[:, r - k - 128 :]
                a_ref[r : r + 128, r:] -= full_dot(below, right, ((0,), (0,)))
            x_ref[k + 128 :, :] -= full_dot(u, x, ((0,), (0,)))


def last_basis_kernel(where_ref, mine_ref, other_ref, image_ref, out_ref, x_ref, a_ref, row_ref):
    load_gram(where_ref, mine_ref, other_ref, a_ref)
    x_ref[...] = image_ref[...]
    solve(x_ref, a_ref, row_ref)
    out_ref[...] = x_ref[rows_of(where_ref[2] * 4 + where_ref[3], out_ref.shape[0]), :].astype(out_ref.dtype)


def last_basis(where, mine, other, image):
    n = mine.shape[2]
    outputs = [array((2 * mine.shape[1], image.shape[1]), jnp.bfloat16)]
    scratch = [pltpu.VMEM(image.shape, jnp.float32), pltpu.VMEM((n, n), jnp.float32), pltpu.VMEM((64, 128), jnp.float32)]
    return on_chip(last_basis_kernel, outputs, scratch, 200 * n**3, "last_basis")(where, mine, other, image)[0]


def put_in_order(where_ref, pieces, block_ref):
    width = pieces[0].shape[1]
    for m, piece in enumerate(pieces):
        for a in range(2):
            block_ref[rows_of(behind(where_ref[2], where_ref[3], a, m), width), :] = piece[a]


def gram_rows(where_ref, block_ref, part_ref, keep_ref, give_ref):
    half = keep_ref.shape[0]
    core = where_ref[4]
    mine = block_ref[rows_of(where_ref[2] * 4 + where_ref[3], 2 * half), :]
    part_ref[...] = full_dot(mine, block_ref[...], ((1,), (1,)))
    keep_ref[...] = part_ref[rows_of(core, half), :]
    give_ref[...] = part_ref[rows_of(1 - core, half), :]


def gram_kernel(where_ref, *refs):
    keep_ref, give_ref, block_ref, part_ref = refs[4:]
    put_in_order(where_ref, refs[:4], block_ref)
    gram_rows(where_ref, block_ref, part_ref, keep_ref, give_ref)


def gram_terms(where, pieces):
    width, features = pieces[0].shape[1:]
    n = 8 * width
    outputs = [array((width // 2, n))] * 2
    scratch = [pltpu.VMEM((n, features), jnp.float32), pltpu.VMEM((width, n), jnp.float32)]
    return on_chip(gram_kernel, outputs, scratch, 2 * 10**9, "gram_terms")(where, *pieces)


def add_kernel(where_ref, *refs):
    pieces, out_ref, terms_ref = refs[:4], refs[4], refs[5]
    for m, piece in enumerate(pieces):
        terms_ref[behind(0, where_ref[1], 0, m)] = piece[...]
    total = sum(terms_ref[i] for i in range(4))
    for i in range(8):
        out_ref[i] = total


def add_in_order(where, pieces):
    shape = pieces[0].shape
    return on_chip(add_kernel, [array((8,) + shape)], [pltpu.VMEM((4,) + shape, jnp.float32)], 10**9, "add_in_order")(
        where, *pieces
    )[0]


def add_both_kernel(scale, where_ref, x_ref, out_ref):
    width = out_ref.shape[1] // 2
    quarter = width // 4
    product = sum(x_ref[i, :width] for i in range(8)) * scale
    for ring in range(2):
        gram = sum(x_ref[4 * ring + i, width:] for i in range(4))
        for i in range(8):
            for j in range(2):
                at = width + (2 * j + ring) * quarter
                out_ref[i, at : at + quarter] = gram[j * quarter : (j + 1) * quarter]
    for i in range(8):
        out_ref[i, :width] = product


def add_both(where, x, scale):
    kernel = functools.partial(add_both_kernel, scale)
    blocks, rows, features = x.shape
    return on_chip(kernel, [array((blocks, rows // 3 * 4, features))], [], 10**9, "add_both")(where, x)[0]


def normalised_kernel(where_ref, mine_ref, other_ref, image_ref, keep_ref, give_ref, a_ref, row_ref, part_ref):
    blocks, width, features = mine_ref.shape
    width //= 2
    half = width // 2
    core = where_ref[4]
    for i in range(blocks):
        image_ref[rows_of(i, width), :] = mine_ref[i, :width]
        for j in range(2):
            at = slice(width + j * half, width + (j + 1) * half)
            columns = slice(j * features, (j + 1) * features)
            a_ref[rows_of(2 * i + core, half), columns] = mine_ref[i, at]
            a_ref[rows_of(2 * i + 1 - core, half), columns] = other_ref[i, at]
    solve(image_ref, a_ref, row_ref)
    gram_rows(where_ref, image_ref, part_ref, keep_ref, give_ref)


def normalised(where, mine, other):
    _, width, features = mine.shape
    width //= 2
    n = 8 * width
    outputs = [array((n, features)), array((width // 2, n)), array((width // 2, n))]
    scratch = [pltpu.VMEM(shape, jnp.float32) for shape in ((n, n), (64, 128), (width, n))]
    return on_chip(normalised_kernel, outputs, scratch, 200 * n**3, "normalised")(where, mine, other)


PIECES = [(0, 0, 2), (1, 0, 2), (2, 0, 2), (3, 0, 2), (4, 0, 2), (5, 0, 2), (6, 0, 2), (7, 0, 1), (7, 1, 1)]
BLOCKS = 8


def three_parts(x):
    high = x.astype(jnp.bfloat16)
    rest = x - high.astype(jnp.float32)
    middle = rest.astype(jnp.bfloat16)
    low = (rest - middle.astype(jnp.float32)).astype(jnp.bfloat16)
    return jnp.concatenate([high, middle, low], 0)


def add_parts(total, width):
    return total[:width] + total[width : 2 * width] + total[2 * width :]


def weights(x):
    return (three_parts(x) if x.dtype == jnp.float32 else x).T


def multiply(pieces, weights_ref, out_ref, blocks=range(8), start_ref=None):
    width, rows = out_ref.shape
    tile = rows // 4
    for quarter in range(4):
        total = 0.0
        for piece, (k, first, count) in zip(pieces, [p for p in PIECES if p[0] in blocks]):
            start = quarter * tile - first * rows // 2
            if 0 <= start < count * rows // 2:
                total += jnp.dot(piece[start : start + tile, :], weights_ref[k], preferred_element_type=jnp.float32)
        total = total.T
        at = slice(quarter * tile, (quarter + 1) * tile)
        total = add_parts(total, width) if len(total) > width else total
        out_ref[:, at] = total if start_ref is None else start_ref[:, at] + total


def first_kernel(blocks, where_ref, *refs):
    basis, pieces, (out_ref, weights_ref, block_ref) = refs[:4], refs[4:-3], refs[-3:]
    for k in blocks:
        block = behind(where_ref[2], where_ref[3], k // 4, k % 4)
        for m in range(4):
            part = basis[m][block]
            block_ref[rows_of(behind(0, where_ref[1], 0, m), part.shape[0]), :] = part
        weights_ref[k] = weights(block_ref[...])
    if blocks[0] == 0:
        multiply(pieces, weights_ref, out_ref, blocks)
    else:
        multiply(pieces[1:], weights_ref, out_ref, blocks, pieces[0])


def load_from_rows(where_ref, basis, weights_ref):
    for m in range(4):
        for a in range(2):
            block = behind(where_ref[0], where_ref[1], a, m)
            step = lax.rem(where_ref[3] + 4 - lax.rem(block, 4), 4)
            place = (lax.div(block, 4) ^ where_ref[2]) * 4 + gray(step)
            weights_ref[place] = weights(basis[m][a])


def next_kernel(where_ref, *refs):
    pieces, out_ref, weights_ref = refs[4 : 4 + len(PIECES)], refs[-2], refs[-1]
    load_from_rows(where_ref, refs[:4], weights_ref)
    multiply(pieces, weights_ref, out_ref)


def compressed_kernel(where_ref, *refs):
    pieces, (keep_ref, give_ref, weights_ref, out_ref) = refs[4:-4], refs[-4:]
    load_from_rows(where_ref, refs[:4], weights_ref)
    multiply(pieces, weights_ref, out_ref)
    half = keep_ref.shape[0]
    core = where_ref[4]
    keep_ref[...] = out_ref[rows_of(core, half), :]
    give_ref[...] = out_ref[rows_of(1 - core, half), :]


def product_flops(rows, width, features):
    return 16 * rows * width * BLOCKS * features


def first_product(where, basis, pieces):
    features = basis[0].shape[2]
    width = 4 * basis[0].shape[1]
    rows = pieces[0].shape[0]
    scratch = [pltpu.VMEM((BLOCKS, features, 3 * width), jnp.bfloat16), pltpu.VMEM((width, features), jnp.float32)]
    flops = product_flops(rows, width, features)
    outputs = [array((width, rows))]
    early = sum(k < BLOCKS - 1 for k, _, _ in PIECES)
    kernel = functools.partial(first_kernel, range(BLOCKS - 1))
    out = on_chip(kernel, outputs, scratch, flops, "first_product")(where, *basis, *pieces[:early])[0]
    kernel = functools.partial(first_kernel, range(BLOCKS - 1, BLOCKS))
    return on_chip(kernel, outputs, scratch, flops // 8, "first_product_end")(where, *basis, out, *pieces[early:])[0]


def next_product(where, basis, pieces, after):
    width, features = basis[0].shape[1:]
    rows = pieces[0].shape[0]
    scratch = [pltpu.VMEM((BLOCKS, features, 3 * width), jnp.bfloat16)]
    return on_chip(next_kernel, [array((width, rows))], scratch, product_flops(rows, width, features), "next_product")(
        where, *basis, *pieces, after=after
    )[0]


def compress(where, basis, pieces):
    width, features = basis[0].shape[1:]
    rows = pieces[0].shape[0]
    outputs = [array((width // 2, rows))] * 2
    scratch = [pltpu.VMEM((BLOCKS, features, width), jnp.bfloat16), pltpu.VMEM((width, rows), jnp.float32)]
    return on_chip(compressed_kernel, outputs, scratch, product_flops(rows, width, features), "compress")(
        where, *basis, *pieces
    )


def back_kernel(where_ref, mine_ref, other_ref, *refs):
    pieces, outs, (sums_ref, parts_ref) = refs[:-6], refs[-6:-2], refs[-2:]
    width, rows = mine_ref.shape
    parts_ref[...] = three_parts(mine_ref[...] + other_ref[...])
    for block in range(BLOCKS):
        total = 0.0
        for piece, (k, first, count) in zip(pieces, PIECES):
            if k == block:
                at = slice(first * rows // 2, (first + count) * rows // 2)
                total += jnp.dot(parts_ref[:, at], piece[...], preferred_element_type=jnp.float32)
        target = behind(where_ref[2], where_ref[3], block // 4, block % 4)
        step = lax.rem(lax.rem(target, 4) + 4 - where_ref[1], 4)
        sums_ref[gray(step) * 2 + (lax.div(target, 4) ^ where_ref[0])] = add_parts(total, width)
    for m in range(4):
        outs[m][...] = sums_ref[2 * m : 2 * m + 2]


def back_and_gram_kernel(where_ref, mine_ref, other_ref, gram_ref, *refs):
    pieces, (out_ref, parts_ref) = refs[:-2], refs[-2:]
    width, rows = mine_ref.shape
    features = out_ref.shape[2]
    quarter = width // 4
    gram = gram_ref[rows_of(where_ref[0], quarter), :]
    for i in range(BLOCKS):
        for j in range(2):
            at = slice(width + j * quarter, width + (j + 1) * quarter)
            out_ref[i, at] = gram[:, j * features : (j + 1) * features]
    parts_ref[...] = three_parts(mine_ref[...] + other_ref[...])
    for block in range(BLOCKS):
        total = 0.0
        for piece, (k, first, count) in zip(pieces, PIECES):
            if k == block:
                at = slice(first * rows // 2, (first + count) * rows // 2)
                total += jnp.dot(parts_ref[:, at], piece[...], preferred_element_type=jnp.float32)
        target = behind(where_ref[2], where_ref[3], block // 4, block % 4)
        out_ref[target, :width] = add_parts(total, width)


def back_and_gram(where, mine, other, gram, pieces):
    width, rows = mine.shape
    features = pieces[0].shape[1]
    outputs = [array((BLOCKS, width * 3 // 2, features))]
    scratch = [pltpu.VMEM((3 * width, rows), jnp.bfloat16)]
    return on_chip(back_and_gram_kernel, outputs, scratch, product_flops(rows, width, features), "back_and_gram")(
        where, mine, other, gram, *pieces
    )[0]


def back_product(where, mine, other, pieces):
    width, rows = mine.shape
    features = pieces[0].shape[1]
    outputs = [array((2, width, features))] * 4
    scratch = [pltpu.VMEM((BLOCKS, width, features), jnp.float32), pltpu.VMEM((3 * width, rows), jnp.bfloat16)]
    return on_chip(back_kernel, outputs, scratch, product_flops(rows, width, features), "back_product")(
        where, mine, other, *pieces
    )


def exchange(x, axes):
    return lax.all_to_all(x, axes, 0, 0, tiled=True)


def swap(x, axis):
    return lax.ppermute(x, axis, [(0, 1), (1, 0)])


def shift(x, axis, step):
    return lax.ppermute(x, axis, [(i, (i + step) % 4) for i in range(4)])


def fan_out(x, axes):
    outer, inner = axes
    pair = jnp.stack([x, swap(x, outer)])
    return [pair] + [shift(pair, inner, GRAY[m]) for m in (1, 2, 3)]


def fan_in(pairs, axes):
    outer, inner = axes
    pair = pairs[0] + sum(shift(pairs[m], inner, GRAY[m]) for m in (1, 2, 3))
    return pair[0] + swap(pair[1], outer)


def gather_all(where, x, start_basis):
    features, n = start_basis.shape
    mine = lax.dynamic_index_in_dim(start_basis.reshape(features, 8, 4, n // 32), where[1], 2, False)
    basis = exchange(mine.transpose(1, 2, 0), PLANE)
    half = x.shape[0] // 2
    before, after = shift(x, "z", 1), shift(x, "z", 3)
    across = swap(x, "y_lo")
    before, _ = hold(where, before, (after, basis))
    basis = [basis] + [shift(basis, "x", GRAY[m]) for m in (1, 2, 3)]
    far = shift(before, "z", 1)
    across_before = swap(before, "y_lo")
    across_after = shift(across, "z", 3)
    far, far_half = hold(where, far, (basis[1], basis[2], basis[3]))
    far_top = swap(far_half, "y_lo")
    far_low = shift(across_after[half:], "z", 3)
    return [hold(where, x)[0], before, after, far, across, across_before, across_after, far_top, far_low], basis


def whole_gram(where, part):
    part = part + swap(part, "y_hi")
    pieces = [part] + [shift(part, "x", GRAY[m]) for m in (1, 2, 3)]
    part = exchange(add_in_order(where, pieces), PLANE)
    return part, swap(part, "core")


def local(entities, start_basis):
    total_rows = entities.shape[0] * lax.axis_size(ROWS)
    where = jnp.stack([lax.axis_index(a) for a in ROWS + COLS]).astype(jnp.int32)

    pieces, basis = gather_all(where, entities, start_basis)

    image = first_product(where, basis, pieces)
    image = fan_in(back_product(where, image, swap(image, "core"), pieces), ROWS) / total_rows
    keep, give = gram_terms(where, fan_out(image, PLANE))
    part = keep + swap(give, "core")
    for step in range(1, ITERS):
        product = next_product(where, fan_out(image, ROWS), pieces, [part])
        sent = back_and_gram(where, product, swap(product, "core"), part + swap(part, "y_hi"), pieces)
        both = exchange(add_both(where, exchange(sent, ROWS), 1.0 / total_rows), PLANE)
        block, keep, give = normalised(where, both, swap(both, "core"))
        part = keep + swap(give, "core")
    rounded = last_basis(where, *whole_gram(where, part), block)
    keep, give = compress(where, fan_out(rounded, ROWS), pieces)
    return (keep + swap(give, "core")).T.astype(jnp.bfloat16)


def solution(mesh):
    fine = Mesh(mesh.devices.reshape(2, 4, 2, 4, 2), ROWS + COLS)
    return jax.shard_map(
        local,
        mesh=fine,
        in_specs=(P(ROWS, COLS), P(COLS, None)),
        out_specs=P(ROWS, COLS),
        check_vma=False,
    )
```

```python
import functools

import jax
import jax.numpy as jnp
from jax import lax
from jax.experimental import pallas as pl
from jax.experimental.pallas import tpu as pltpu
from jax.sharding import Mesh, PartitionSpec as P

ITERS = 2
ROWS = ("y_hi", "x")
PLANE = ("y_lo", "z")
COLS = ("y_lo", "z", "core")
HIGHEST = lax.Precision.HIGHEST
VMEM_LIMIT = 16 * 2**20
MIDDLE = 64


def full_dot(a, b, contract):
    return lax.dot_general(
        a, b, (contract, ((), ())), precision=HIGHEST, preferred_element_type=jnp.float32
    )


def spread(x):
    return jnp.broadcast_to(x, (8, 128))


def eliminate(left, right, col, row_ref):
    slot = col // 8 % 4 * 16
    row_ref[slot : slot + 8, :] = left[0]
    row_ref[slot + 8 : slot + 16, :] = right[0]
    rows_left = [row_ref[pl.ds(slot + i, 8, stride=0), :] for i in range(8)]
    rows_right = [row_ref[pl.ds(slot + 8 + i, 8, stride=0), :] for i in range(8)]
    s = [[spread(rows_left[i][:, col + j : col + j + 1]) if j >= i else None for j in range(8)] for i in range(8)]
    inverse = []
    for j in range(8):
        inverse.append(1.0 / s[j][j])
        for i in range(j + 1, 8):
            factor = s[j][i] * inverse[j]
            for k in range(i, 8):
                s[i][k] = s[i][k] - factor * s[j][k]
            rows_left[i] = rows_left[i] - factor * rows_left[j]
            rows_right[i] = rows_right[i] - factor * rows_right[j]
    row = lax.broadcasted_iota(jnp.int32, (8, 128), 0)
    done_left, done_right, scale = rows_left[0], rows_right[0], inverse[0]
    for i in range(1, 8):
        done_left = jnp.where(row == i, rows_left[i], done_left)
        done_right = jnp.where(row == i, rows_right[i], done_right)
        scale = jnp.where(row == i, inverse[i], scale)
    new_left, new_right = [], []
    for x, y in zip(left[1:], right[1:]):
        c = [spread(x[:, col + j : col + j + 1]) for j in range(8)]
        for j in range(8):
            factor = c[j] * inverse[j]
            for k in range(j + 1, 8):
                c[k] = c[k] - factor * s[j][k]
            x = x - factor * rows_left[j]
            y = y - factor * rows_right[j]
        new_left.append(x)
        new_right.append(y)
    return done_left, done_right, scale, new_left, new_right


def invert_block(a, row_ref):
    rows = lax.broadcasted_iota(jnp.int32, (128, 128), 0)
    cols = lax.broadcasted_iota(jnp.int32, (128, 128), 1)
    v = jnp.where(rows == cols, 1.0, 0.0).astype(jnp.float32)
    out = []
    for m in range(0, 128, MIDDLE):
        left = [a[i : i + 8, :] for i in range(0, MIDDLE, 8)]
        right = [v[i : i + 8, :] for i in range(0, MIDDLE, 8)]
        lefts, rights, scales = [], [], []
        for g in range(MIDDLE // 8):
            done_left, done_right, scale, left, right = eliminate(left, right, m + 8 * g, row_ref)
            lefts.append(done_left)
            rights.append(done_right)
            scales.append(scale)
        u, w, d = jnp.concatenate(lefts, 0), jnp.concatenate(rights, 0), jnp.concatenate(scales, 0)
        out.append(w * jnp.sqrt(d))
        if m + MIDDLE < 128:
            factors = (u * d)[:, m + MIDDLE :]
            a = a[MIDDLE:] - full_dot(factors, u, ((0,), (0,)))
            v = v[MIDDLE:] - full_dot(factors, w, ((0,), (0,)))
    return jnp.concatenate(out, 0)


IN_VMEM = pl.BlockSpec(memory_space=pltpu.VMEM)
IN_SMEM = pl.BlockSpec(memory_space=pltpu.SMEM)
ANYWHERE = pl.BlockSpec(memory_space=pl.ANY)


def on_chip(kernel, outputs, scratch, flops, name):
    def call(where, *operands, after=()):
        return pl.pallas_call(
            kernel,
            out_shape=outputs,
            in_specs=[IN_SMEM] + [IN_VMEM] * len(operands) + [ANYWHERE] * len(after),
            out_specs=[IN_VMEM] * len(outputs),
            scratch_shapes=scratch,
            compiler_params=pltpu.CompilerParams(vmem_limit_bytes=VMEM_LIMIT),
            cost_estimate=pl.CostEstimate(flops=flops, bytes_accessed=2**20, transcendentals=0),
            name=name,
        )(where, *operands, *after)

    return call


def hold_kernel(where_ref, x_ref, *refs):
    out_ref, top_ref = refs[-2:]
    out_ref[...] = x_ref[...]
    top_ref[...] = x_ref[: top_ref.shape[0], :]


def hold(where, x, after=()):
    outputs = [array(x.shape, x.dtype), array((x.shape[0] // 2, x.shape[1]), x.dtype)]
    return on_chip(hold_kernel, outputs, [], 10**9, "hold")(where, x, after=after)


def array(shape, dtype=jnp.float32):
    return jax.ShapeDtypeStruct(shape, dtype)


GRAY = (0, 1, 3, 2)


def gray(step):
    return step ^ lax.shift_right_logical(step, 1)


def behind(outer, inner, a, m):
    return (outer ^ a) * 4 + lax.rem(inner + 4 - GRAY[m], 4)


def rows_of(block, width):
    return pl.ds(pl.multiple_of(block * width, 8), width)


def load_gram(where_ref, mine_ref, other_ref, a_ref):
    core = where_ref[4]
    blocks, half = mine_ref.shape[:2]
    for i in range(blocks):
        a_ref[rows_of(2 * i + core, half), :] = mine_ref[i]
        a_ref[rows_of(2 * i + 1 - core, half), :] = other_ref[i]


def solve(x_ref, a_ref, row_ref):
    n = a_ref.shape[0]
    for k in range(0, n, 128):
        block = slice(k, k + 128)
        w = invert_block(a_ref[block, block], row_ref)
        x = full_dot(w, x_ref[block, :], ((1,), (0,)))
        x_ref[block, :] = x
        if k + 128 < n:
            u = full_dot(w, a_ref[block, k + 128 :], ((1,), (0,)))
            for r in range(k + 128, n, 128):
                below, right = u[:, r - k - 128 : r - k], u[:, r - k - 128 :]
                a_ref[r : r + 128, r:] -= full_dot(below, right, ((0,), (0,)))
            x_ref[k + 128 :, :] -= full_dot(u, x, ((0,), (0,)))


def last_basis_kernel(where_ref, mine_ref, other_ref, image_ref, out_ref, x_ref, a_ref, row_ref):
    load_gram(where_ref, mine_ref, other_ref, a_ref)
    x_ref[...] = image_ref[...]
    solve(x_ref, a_ref, row_ref)
    out_ref[...] = x_ref[rows_of(where_ref[2] * 4 + where_ref[3], out_ref.shape[0]), :].astype(out_ref.dtype)


def last_basis(where, mine, other, image):
    n = mine.shape[2]
    outputs = [array((2 * mine.shape[1], image.shape[1]), jnp.bfloat16)]
    scratch = [pltpu.VMEM(image.shape, jnp.float32), pltpu.VMEM((n, n), jnp.float32), pltpu.VMEM((64, 128), jnp.float32)]
    return on_chip(last_basis_kernel, outputs, scratch, 200 * n**3, "last_basis")(where, mine, other, image)[0]


def put_in_order(where_ref, pieces, block_ref):
    width = pieces[0].shape[1]
    for m, piece in enumerate(pieces):
        for a in range(2):
            block_ref[rows_of(behind(where_ref[2], where_ref[3], a, m), width), :] = piece[a]


def gram_rows(where_ref, block_ref, part_ref, keep_ref, give_ref):
    half = keep_ref.shape[0]
    core = where_ref[4]
    mine = block_ref[rows_of(where_ref[2] * 4 + where_ref[3], 2 * half), :]
    part_ref[...] = full_dot(mine, block_ref[...], ((1,), (1,)))
    keep_ref[...] = part_ref[rows_of(core, half), :]
    give_ref[...] = part_ref[rows_of(1 - core, half), :]


def gram_kernel(where_ref, *refs):
    keep_ref, give_ref, block_ref, part_ref = refs[4:]
    put_in_order(where_ref, refs[:4], block_ref)
    gram_rows(where_ref, block_ref, part_ref, keep_ref, give_ref)


def gram_terms(where, pieces):
    width, features = pieces[0].shape[1:]
    n = 8 * width
    outputs = [array((width // 2, n))] * 2
    scratch = [pltpu.VMEM((n, features), jnp.float32), pltpu.VMEM((width, n), jnp.float32)]
    return on_chip(gram_kernel, outputs, scratch, 2 * 10**9, "gram_terms")(where, *pieces)


def add_kernel(where_ref, *refs):
    pieces, out_ref, terms_ref = refs[:4], refs[4], refs[5]
    for m, piece in enumerate(pieces):
        terms_ref[behind(0, where_ref[1], 0, m)] = piece[...]
    total = sum(terms_ref[i] for i in range(4))
    for i in range(8):
        out_ref[i] = total


def add_in_order(where, pieces):
    shape = pieces[0].shape
    return on_chip(add_kernel, [array((8,) + shape)], [pltpu.VMEM((4,) + shape, jnp.float32)], 10**9, "add_in_order")(
        where, *pieces
    )[0]


def add_both_kernel(scale, where_ref, x_ref, out_ref):
    width = out_ref.shape[1] // 2
    quarter = width // 4
    product = sum(x_ref[i, :width] for i in range(8)) * scale
    for ring in range(2):
        gram = sum(x_ref[4 * ring + i, width:] for i in range(4))
        for i in range(8):
            for j in range(2):
                at = width + (2 * j + ring) * quarter
                out_ref[i, at : at + quarter] = gram[j * quarter : (j + 1) * quarter]
    for i in range(8):
        out_ref[i, :width] = product


def add_both(where, x, scale):
    kernel = functools.partial(add_both_kernel, scale)
    blocks, rows, features = x.shape
    return on_chip(kernel, [array((blocks, rows // 3 * 4, features))], [], 10**9, "add_both")(where, x)[0]


def normalised_kernel(where_ref, mine_ref, other_ref, image_ref, keep_ref, give_ref, a_ref, row_ref, part_ref):
    blocks, width, features = mine_ref.shape
    width //= 2
    half = width // 2
    core = where_ref[4]
    for i in range(blocks):
        image_ref[rows_of(i, width), :] = mine_ref[i, :width]
        for j in range(2):
            at = slice(width + j * half, width + (j + 1) * half)
            columns = slice(j * features, (j + 1) * features)
            a_ref[rows_of(2 * i + core, half), columns] = mine_ref[i, at]
            a_ref[rows_of(2 * i + 1 - core, half), columns] = other_ref[i, at]
    solve(image_ref, a_ref, row_ref)
    gram_rows(where_ref, image_ref, part_ref, keep_ref, give_ref)


def normalised(where, mine, other):
    _, width, features = mine.shape
    width //= 2
    n = 8 * width
    outputs = [array((n, features)), array((width // 2, n)), array((width // 2, n))]
    scratch = [pltpu.VMEM(shape, jnp.float32) for shape in ((n, n), (64, 128), (width, n))]
    return on_chip(normalised_kernel, outputs, scratch, 200 * n**3, "normalised")(where, mine, other)


PIECES = [(0, 0, 2), (1, 0, 2), (2, 0, 2), (3, 0, 2), (4, 0, 2), (5, 0, 2), (6, 0, 2), (7, 0, 1), (7, 1, 1)]
BLOCKS = 8


def three_parts(x):
    high = x.astype(jnp.bfloat16)
    rest = x - high.astype(jnp.float32)
    middle = rest.astype(jnp.bfloat16)
    low = (rest - middle.astype(jnp.float32)).astype(jnp.bfloat16)
    return jnp.concatenate([high, middle, low], 0)


def add_parts(total, width):
    return total[:width] + total[width : 2 * width] + total[2 * width :]


def weights(x):
    return (three_parts(x) if x.dtype == jnp.float32 else x).T


def multiply(pieces, weights_ref, out_ref, blocks=range(8), start_ref=None):
    width, rows = out_ref.shape
    tile = rows // 4
    for quarter in range(4):
        total = 0.0
        for piece, (k, first, count) in zip(pieces, [p for p in PIECES if p[0] in blocks]):
            start = quarter * tile - first * rows // 2
            if 0 <= start < count * rows // 2:
                total += jnp.dot(piece[start : start + tile, :], weights_ref[k], preferred_element_type=jnp.float32)
        total = total.T
        at = slice(quarter * tile, (quarter + 1) * tile)
        total = add_parts(total, width) if len(total) > width else total
        out_ref[:, at] = total if start_ref is None else start_ref[:, at] + total


def first_kernel(blocks, where_ref, *refs):
    basis, pieces, (out_ref, weights_ref, block_ref) = refs[:4], refs[4:-3], refs[-3:]
    for k in blocks:
        block = behind(where_ref[2], where_ref[3], k // 4, k % 4)
        for m in range(4):
            part = basis[m][block]
            block_ref[rows_of(behind(0, where_ref[1], 0, m), part.shape[0]), :] = part
        weights_ref[k] = weights(block_ref[...])
    if blocks[0] == 0:
        multiply(pieces, weights_ref, out_ref, blocks)
    else:
        multiply(pieces[1:], weights_ref, out_ref, blocks, pieces[0])


def load_from_rows(where_ref, basis, weights_ref):
    for m in range(4):
        for a in range(2):
            block = behind(where_ref[0], where_ref[1], a, m)
            step = lax.rem(where_ref[3] + 4 - lax.rem(block, 4), 4)
            place = (lax.div(block, 4) ^ where_ref[2]) * 4 + gray(step)
            weights_ref[place] = weights(basis[m][a])


def next_kernel(where_ref, *refs):
    pieces, out_ref, weights_ref = refs[4 : 4 + len(PIECES)], refs[-2], refs[-1]
    load_from_rows(where_ref, refs[:4], weights_ref)
    multiply(pieces, weights_ref, out_ref)


def compressed_kernel(where_ref, *refs):
    pieces, (keep_ref, give_ref, weights_ref, out_ref) = refs[4:-4], refs[-4:]
    load_from_rows(where_ref, refs[:4], weights_ref)
    multiply(pieces, weights_ref, out_ref)
    half = keep_ref.shape[0]
    core = where_ref[4]
    keep_ref[...] = out_ref[rows_of(core, half), :]
    give_ref[...] = out_ref[rows_of(1 - core, half), :]


def product_flops(rows, width, features):
    return 16 * rows * width * BLOCKS * features


def first_product(where, basis, pieces):
    features = basis[0].shape[2]
    width = 4 * basis[0].shape[1]
    rows = pieces[0].shape[0]
    scratch = [pltpu.VMEM((BLOCKS, features, 3 * width), jnp.bfloat16), pltpu.VMEM((width, features), jnp.float32)]
    flops = product_flops(rows, width, features)
    outputs = [array((width, rows))]
    early = sum(k < BLOCKS - 1 for k, _, _ in PIECES)
    kernel = functools.partial(first_kernel, range(BLOCKS - 1))
    out = on_chip(kernel, outputs, scratch, flops, "first_product")(where, *basis, *pieces[:early])[0]
    kernel = functools.partial(first_kernel, range(BLOCKS - 1, BLOCKS))
    return on_chip(kernel, outputs, scratch, flops // 8, "first_product_end")(where, *basis, out, *pieces[early:])[0]


def next_product(where, basis, pieces, after):
    width, features = basis[0].shape[1:]
    rows = pieces[0].shape[0]
    scratch = [pltpu.VMEM((BLOCKS, features, 3 * width), jnp.bfloat16)]
    return on_chip(next_kernel, [array((width, rows))], scratch, product_flops(rows, width, features), "next_product")(
        where, *basis, *pieces, after=after
    )[0]


def compress(where, basis, pieces):
    width, features = basis[0].shape[1:]
    rows = pieces[0].shape[0]
    outputs = [array((width // 2, rows))] * 2
    scratch = [pltpu.VMEM((BLOCKS, features, width), jnp.bfloat16), pltpu.VMEM((width, rows), jnp.float32)]
    return on_chip(compressed_kernel, outputs, scratch, product_flops(rows, width, features), "compress")(
        where, *basis, *pieces
    )


def back_kernel(where_ref, mine_ref, other_ref, *refs):
    pieces, outs, (sums_ref, parts_ref) = refs[:-6], refs[-6:-2], refs[-2:]
    width, rows = mine_ref.shape
    parts_ref[...] = three_parts(mine_ref[...] + other_ref[...])
    for block in range(BLOCKS):
        total = 0.0
        for piece, (k, first, count) in zip(pieces, PIECES):
            if k == block:
                at = slice(first * rows // 2, (first + count) * rows // 2)
                total += jnp.dot(parts_ref[:, at], piece[...], preferred_element_type=jnp.float32)
        target = behind(where_ref[2], where_ref[3], block // 4, block % 4)
        step = lax.rem(lax.rem(target, 4) + 4 - where_ref[1], 4)
        sums_ref[gray(step) * 2 + (lax.div(target, 4) ^ where_ref[0])] = add_parts(total, width)
    for m in range(4):
        outs[m][...] = sums_ref[2 * m : 2 * m + 2]


def back_and_gram_kernel(where_ref, mine_ref, other_ref, gram_ref, *refs):
    pieces, (out_ref, parts_ref) = refs[:-2], refs[-2:]
    width, rows = mine_ref.shape
    features = out_ref.shape[2]
    quarter = width // 4
    gram = gram_ref[rows_of(where_ref[0], quarter), :]
    for i in range(BLOCKS):
        for j in range(2):
            at = slice(width + j * quarter, width + (j + 1) * quarter)
            out_ref[i, at] = gram[:, j * features : (j + 1) * features]
    parts_ref[...] = three_parts(mine_ref[...] + other_ref[...])
    for block in range(BLOCKS):
        total = 0.0
        for piece, (k, first, count) in zip(pieces, PIECES):
            if k == block:
                at = slice(first * rows // 2, (first + count) * rows // 2)
                total += jnp.dot(parts_ref[:, at], piece[...], preferred_element_type=jnp.float32)
        target = behind(where_ref[2], where_ref[3], block // 4, block % 4)
        out_ref[target, :width] = add_parts(total, width)


def back_and_gram(where, mine, other, gram, pieces):
    width, rows = mine.shape
    features = pieces[0].shape[1]
    outputs = [array((BLOCKS, width * 3 // 2, features))]
    scratch = [pltpu.VMEM((3 * width, rows), jnp.bfloat16)]
    return on_chip(back_and_gram_kernel, outputs, scratch, product_flops(rows, width, features), "back_and_gram")(
        where, mine, other, gram, *pieces
    )[0]


def back_product(where, mine, other, pieces):
    width, rows = mine.shape
    features = pieces[0].shape[1]
    outputs = [array((2, width, features))] * 4
    scratch = [pltpu.VMEM((BLOCKS, width, features), jnp.float32), pltpu.VMEM((3 * width, rows), jnp.bfloat16)]
    return on_chip(back_kernel, outputs, scratch, product_flops(rows, width, features), "back_product")(
        where, mine, other, *pieces
    )


def exchange(x, axes):
    return lax.all_to_all(x, axes, 0, 0, tiled=True)


def swap(x, axis):
    return lax.ppermute(x, axis, [(0, 1), (1, 0)])


def shift(x, axis, step):
    return lax.ppermute(x, axis, [(i, (i + step) % 4) for i in range(4)])


def around(pair, inner):
    return [pair] + [shift(pair, inner, GRAY[m]) for m in (1, 2, 3)]


def fan_out(x, axes):
    outer, inner = axes
    return around(jnp.stack([x, swap(x, outer)]), inner)


def fan_in(pairs, axes):
    outer, inner = axes
    pair = pairs[0] + sum(shift(pairs[m], inner, GRAY[m]) for m in (1, 2, 3))
    other = swap(pair, outer)
    return jnp.stack([pair[0] + other[1], pair[1] + other[0]])


def gather_all(where, x, start_basis):
    features, n = start_basis.shape
    mine = lax.dynamic_index_in_dim(start_basis.reshape(features, 8, 4, n // 32), where[1], 2, False)
    basis = exchange(mine.transpose(1, 2, 0), PLANE)
    half = x.shape[0] // 2
    before, after = shift(x, "z", 1), shift(x, "z", 3)
    across = swap(x, "y_lo")
    before, _ = hold(where, before, (after, basis))
    basis = [basis] + [shift(basis, "x", GRAY[m]) for m in (1, 2, 3)]
    far = shift(before, "z", 1)
    across_before = swap(before, "y_lo")
    across_after = shift(across, "z", 3)
    far, far_half = hold(where, far, (basis[1], basis[2], basis[3]))
    far_top = swap(far_half, "y_lo")
    far_low = shift(across_after[half:], "z", 3)
    return [hold(where, x)[0], before, after, far, across, across_before, across_after, far_top, far_low], basis


def whole_gram(where, part):
    part = part + swap(part, "y_hi")
    pieces = [part] + [shift(part, "x", GRAY[m]) for m in (1, 2, 3)]
    part = exchange(add_in_order(where, pieces), PLANE)
    return part, swap(part, "core")


def local(entities, start_basis):
    total_rows = entities.shape[0] * lax.axis_size(ROWS)
    where = jnp.stack([lax.axis_index(a) for a in ROWS + COLS]).astype(jnp.int32)

    pieces, basis = gather_all(where, entities, start_basis)

    image = first_product(where, basis, pieces)
    images = fan_in(back_product(where, image, swap(image, "core"), pieces), ROWS) / total_rows
    keep, give = gram_terms(where, fan_out(images[0], PLANE))
    part = keep + swap(give, "core")
    for step in range(1, ITERS):
        product = next_product(where, around(images, "x"), pieces, [part])
        sent = back_and_gram(where, product, swap(product, "core"), part + swap(part, "y_hi"), pieces)
        both = exchange(add_both(where, exchange(sent, ROWS), 1.0 / total_rows), PLANE)
        block, keep, give = normalised(where, both, swap(both, "core"))
        part = keep + swap(give, "core")
    rounded = last_basis(where, *whole_gram(where, part), block)
    keep, give = compress(where, fan_out(rounded, ROWS), pieces)
    return (keep + swap(give, "core")).T.astype(jnp.bfloat16)


def solution(mesh):
    fine = Mesh(mesh.devices.reshape(2, 4, 2, 4, 2), ROWS + COLS)
    return jax.shard_map(
        local,
        mesh=fine,
        in_specs=(P(ROWS, COLS), P(COLS, None)),
        out_specs=P(ROWS, COLS),
        check_vma=False,
    )
```
